32 devices in a mesh: grp: 2 (over y), ctx: 4 (over x, core), head: 4 (over z).
Axes of the slice: x: 2, y: 2, z: 4, core: 2. Of those that a mesh axis runs over, the one named last changes fastest.
Arguments:
- query_codes: bfloat16 [8192, 2048], P(('grp', 'ctx', 'head')), parts along dimension 0, may hold values from -0.5 to 2.5
- key_codes: bfloat16 [8192, 2048], P(('grp', 'ctx', 'head')), parts along dimension 0, may hold values from -0.5 to 2.5
- value_codes: bfloat16 [8192, 4096], P(('grp', 'ctx', 'head')), parts along dimension 0, may hold values from -6 to 6
- block_scales: float32 [64, 3, 8], P(('grp', 'ctx', 'head')), parts along dimension 0, may hold values from 0.25 to 2
- fault_tensor: int32 [64, 8], P(('grp', 'ctx', 'head')), parts along dimension 0, may hold values from 0 to 2
- fault_offset: int32 [64, 8], P(('grp', 'ctx', 'head')), parts along dimension 0, may hold values from 0 to 65535
- fault_bit: int32 [64, 8], P(('grp', 'ctx', 'head')), parts along dimension 0, may hold values from 0 to 3
- input_gate: bfloat16 [8192, 8], P(('grp', 'ctx', 'head')), parts along dimension 0, may hold values from -10 to 104
- forget_gate: bfloat16 [8192, 8], P(('grp', 'ctx', 'head')), parts along dimension 0, may hold values from 0.5 to 15
Outputs:
- hidden_states: bfloat16 [8192, 4096], P(('grp', 'ctx', 'head')), parts along dimension 0
The draws below stay inside these ranges and needn't reach their ends.
There are 2 independent parts, one for each index of `grp`. The reference program is written for one: setup_inputs(seed, part) draws one part's arguments, and reference() takes and returns one part's arrays. A program takes and returns all parts, laid end to end along the dimension named above; each array names one. Nothing has to cross between parts.
All inputs are finite; a program needn't handle non-finite values.
Results may differ from the reference program's by a relative error of at most 0.0057.
Values may be sent and summed in bfloat16 or wider, within the bound.
A program may use at most 128 MiB of HBM per device.

```python
import math
import jax
import jax.numpy as jnp
from jax import lax

ATTENTION_UNITS = 8
DK = 256
DV = 512
CH = 256
BLK = 128
CONTEXT_LENGTH = 4096
NBLK = 32


def shared_codes(key):
    spanwise_outcome = 0.5 * jnp.clip(jax.random.normal(key, (CONTEXT_LENGTH, ATTENTION_UNITS * DK)), -3.0, 3.0)
    return (1.0 + spanwise_outcome).astype(jnp.bfloat16)


def draw_query_codes(key, part):
    return shared_codes(jax.random.fold_in(key, 11))


def draw_key_codes(key, part):
    return shared_codes(jax.random.fold_in(key, 23))


def draw_input_gate(key, part):
    return jnp.clip(-2.0 + 1.5 * jax.random.normal(key, (CONTEXT_LENGTH, ATTENTION_UNITS)), -10.0, 6.0).astype(jnp.bfloat16)


def draw_forget_gate(key, part):
    lookup_vectors = jax.random.split(key, 6)
    order = jax.random.permutation(lookup_vectors[0], ATTENTION_UNITS)
    quick = order < ATTENTION_UNITS // 2
    slow_base = jnp.minimum(math.log(CONTEXT_LENGTH) + 1.0 + jax.random.uniform(lookup_vectors[1], (ATTENTION_UNITS,), minval=0.0, maxval=2.0), 14.0)
    quick_base = math.log(40.0) + jax.random.uniform(lookup_vectors[2], (ATTENTION_UNITS,), minval=-0.3, maxval=0.3)
    drawn_outcome = jnp.where(quick, quick_base, slow_base)
    spanwise_outcome = jax.random.uniform(lookup_vectors[3], (CONTEXT_LENGTH, ATTENTION_UNITS), minval=-0.35, maxval=0.35)
    corruption_positions = jax.random.randint(lookup_vectors[4], (3,), 0, CONTEXT_LENGTH)
    corruption_cluster = jnp.any(jnp.arange(CONTEXT_LENGTH)[:, None] == corruption_positions[None, :], axis=1)
    corruption_cluster_amount = jax.random.uniform(lookup_vectors[5], (CONTEXT_LENGTH, ATTENTION_UNITS), minval=0.7, maxval=1.4)
    return jnp.where(corruption_cluster[:, None], corruption_cluster_amount, drawn_outcome[None, :] + spanwise_outcome).astype(jnp.bfloat16)


def touch_ends(values, key, least, top_value):
    index_at = [jax.random.randint(jax.random.fold_in(key, axis), (), 0, length) for axis, length in enumerate(values.shape)]
    main_axis = values.shape.index(max(values.shape))
    beside = index_at[:main_axis] + [(index_at[main_axis] + 1) % values.shape[main_axis]] + index_at[main_axis + 1:]
    return values.at[tuple(index_at)].set(least).at[tuple(beside)].set(top_value)


def shard_levels(stream_key, shape, cuts, smallest, top_value):
    level = 1.0
    for axis_at, blocks in cuts:
        heights = jax.random.uniform(jax.random.fold_in(jax.random.fold_in(stream_key, 6), axis_at), (blocks,), jnp.float32, smallest / len(cuts), top_value / len(cuts))
        level = level * jnp.repeat(jnp.exp(heights), shape[axis_at] // blocks).reshape((-1,) + (1,) * (len(shape) - 1 - axis_at))
    return level


def bell_draw(stream_key, shape, scale, bound, cuts=(), kind=jnp.bfloat16):
    values = jax.random.normal(stream_key, shape, jnp.float32) * scale
    if len(cuts) > 0:
        values = shard_levels(stream_key, shape, cuts, -0.22, 0.18) * values
    return jnp.clip(values, min=-bound, max=bound).astype(kind)


def setup_inputs(seed: int = 0, part: int = 0) -> dict:
    key_list = jax.random.split(jax.random.key(seed), 10)
    own_keys = jax.random.split(jax.random.fold_in(key_list[9], part), 10)
    query_codes = draw_query_codes(jax.random.fold_in(jax.random.fold_in(key_list[9], part), 71), part)
    key_codes = draw_key_codes(jax.random.fold_in(jax.random.fold_in(key_list[9], part), 71), part)
    value_codes = bell_draw(own_keys[2], (CONTEXT_LENGTH, ATTENTION_UNITS * DV), 1.0, 6.0, ((0, 16),))
    block_scales = jnp.clip(jnp.exp(math.log(2.0) - 2.0794415 * jax.random.uniform(own_keys[3], (NBLK, 3, ATTENTION_UNITS), jnp.float32) ** shard_levels(own_keys[3], (NBLK, 3, ATTENTION_UNITS), ((0, 16),), -0.2, 0.2)), 0.25, 2.0)
    fault_tensor = touch_ends(jax.random.randint(own_keys[4], (NBLK, ATTENTION_UNITS), 0, 3), jax.random.fold_in(own_keys[4], 1), 0, 2).astype(jnp.int32)
    fault_offset = touch_ends(jax.random.randint(own_keys[5], (NBLK, ATTENTION_UNITS), 0, BLK * DV), jax.random.fold_in(own_keys[5], 1), 0, (BLK * DV) - 1).astype(jnp.int32)
    fault_bit = touch_ends(jax.random.randint(own_keys[6], (NBLK, ATTENTION_UNITS), 0, 4), jax.random.fold_in(own_keys[6], 1), 0, 3).astype(jnp.int32)
    input_gate = draw_input_gate(jax.random.fold_in(jax.random.fold_in(key_list[9], part), 71), part)
    forget_gate = draw_forget_gate(jax.random.fold_in(jax.random.fold_in(key_list[9], part), 71), part)
    return dict(query_codes=query_codes, key_codes=key_codes, value_codes=value_codes, block_scales=block_scales, fault_tensor=fault_tensor, fault_offset=fault_offset, fault_bit=fault_bit, input_gate=input_gate, forget_gate=forget_gate)


NEG_FILL = -1e+30

def dequant(codes, scales, tensor_id, fault_tensor, fault_offset, fault_bit, width):
    rows = codes.shape[0]
    blocks = rows // BLK
    heads = scales.shape[2]
    shaped = codes.reshape(blocks, BLK, heads, width).astype(jnp.float32)
    block_factor = scales[:, tensor_id, :]
    struck = fault_tensor == tensor_id
    token_hit = (fault_offset // DV).astype(jnp.int32)
    column_hit = (fault_offset % DV % width).astype(jnp.int32)
    token_line = jnp.arange(BLK, dtype=jnp.int32)
    column_line = jnp.arange(width, dtype=jnp.int32)
    marked = (token_line[None, :, None, None] == token_hit[:, None, :, None]) & (column_line[None, None, None, :] == column_hit[:, None, :, None]) & struck[:, None, :, None]
    flipped = -jnp.exp2(fault_bit.astype(jnp.float32))
    factor = jnp.where(marked, flipped[:, None, :, None], jnp.ones_like(shaped))
    result = shaped * block_factor[:, None, :, None] * factor
    return result.reshape(rows, heads, width).astype(jnp.bfloat16)

def identity_state(groups):
    return (jnp.zeros((groups, DK, DV), jnp.float32), jnp.zeros((groups, DK), jnp.float32), jnp.full((groups,), NEG_FILL, jnp.float32), jnp.zeros((groups,), jnp.float32))

def combine(earlier, following):
    peak = jnp.maximum(earlier[2] + following[3], following[2])
    first = jnp.exp(earlier[2] + following[3] - peak)
    second = jnp.exp(following[2] - peak)
    matrix = earlier[0] * first[..., None, None] + following[0] * second[..., None, None]
    normer = earlier[1] * first[..., None] + following[1] * second[..., None]
    return (matrix, normer, peak, earlier[3] + following[3])

def span_terms(lookup_vectors, values, gate_in, log_forget):
    running = jnp.cumsum(log_forget, axis=1)
    total = running[:, -1]
    exponent = total[:, None] - running + gate_in
    peak = lax.optimization_barrier(jnp.max(exponent, axis=1))
    weights = jnp.exp(exponent - peak[:, None])
    weighted = lax.optimization_barrier((lookup_vectors.astype(jnp.float32) * weights[..., None]).astype(jnp.bfloat16))
    wide = weighted.astype(jnp.float32)
    matrix = jnp.einsum('csgk,csgv->cgkv', wide, values.astype(jnp.float32))
    normer = lax.optimization_barrier(jnp.sum(wide, axis=1))
    return (matrix, normer, peak, total)

def prefix_states(states, start):

    def advance(carried, element):
        return (combine(carried, element), carried)
    return lax.scan(advance, start, states)

def span_outputs(queries, lookup_vectors, values, gate_in, log_forget, before):
    size = queries.shape[1]
    factor = 1.0 / math.sqrt(DK)
    running = jnp.cumsum(log_forget, axis=1).transpose(0, 2, 1)
    gate_rows = gate_in.transpose(0, 2, 1)
    exponent = running[..., :, None] - running[..., None, :] + gate_rows[..., None, :]
    line = jnp.arange(size, dtype=jnp.int32)
    causal = line[:, None] >= line[None, :]
    exponent = jnp.where(causal, exponent, NEG_FILL)
    inter = running + before[2][..., None]
    row_peak = jnp.maximum(lax.optimization_barrier(jnp.max(exponent, axis=-1)), inter)
    decay = jnp.exp(exponent - row_peak[..., None])
    scores = jnp.einsum('ctgk,csgk->cgts', queries.astype(jnp.float32), lookup_vectors.astype(jnp.float32)) * factor
    product = decay * scores
    product_weights = lax.optimization_barrier(product.astype(jnp.bfloat16))
    numerator = jnp.einsum('cgts,csgv->ctgv', product_weights.astype(jnp.float32), values.astype(jnp.float32))
    lift = jnp.exp(inter - row_peak)
    lifted = lax.optimization_barrier((queries.astype(jnp.float32) * (factor * lift).transpose(0, 2, 1)[..., None]).astype(jnp.bfloat16))
    start_matrix = lax.optimization_barrier(before[0].astype(jnp.bfloat16))
    numerator = numerator + jnp.einsum('ctgk,cgkv->ctgv', lifted.astype(jnp.float32), start_matrix.astype(jnp.float32))
    denominator = lax.optimization_barrier(jnp.sum(product, axis=-1)) + jnp.einsum('ctgk,cgk->cgt', lifted.astype(jnp.float32), before[1], precision=lax.Precision.HIGHEST)
    floor_value = jnp.maximum(jnp.abs(denominator), 1.0)
    return (numerator / floor_value.transpose(0, 2, 1)[..., None]).astype(jnp.bfloat16)

def reference(query_codes, key_codes, value_codes, block_scales, fault_tensor, fault_offset, fault_bit, input_gate, forget_gate):
    queries = dequant(query_codes, block_scales, 0, fault_tensor, fault_offset, fault_bit, DK)
    lookup_vectors = dequant(key_codes, block_scales, 1, fault_tensor, fault_offset, fault_bit, DK)
    values = dequant(value_codes, block_scales, 2, fault_tensor, fault_offset, fault_bit, DV)
    spans = CONTEXT_LENGTH // CH
    log_forget = jax.nn.log_sigmoid(forget_gate.astype(jnp.float32))
    gate_in = input_gate.astype(jnp.float32)

    def split_wide(array):
        return array.reshape(spans, CH, ATTENTION_UNITS, array.shape[2]).transpose(2, 0, 1, 3)[:, :, :, None, :]

    def split_gate(array):
        return array.reshape(spans, CH, ATTENTION_UNITS).transpose(2, 0, 1)[..., None]

    def head_pass(pieces):
        head_q, head_k, head_v, head_i, head_f = pieces
        terms = span_terms(head_k, head_v, head_i, head_f)
        total, before = prefix_states(terms, identity_state(1))
        return span_outputs(head_q, head_k, head_v, head_i, head_f, before)
    outputs = lax.map(head_pass, (split_wide(queries), split_wide(lookup_vectors), split_wide(values), split_gate(gate_in), split_gate(log_forget)))
    return outputs[:, :, :, 0, :].transpose(1, 2, 0, 3).reshape(CONTEXT_LENGTH, ATTENTION_UNITS * DV)
```

```python
import functools
import math

import jax
import jax.numpy as jnp
from jax import lax
from jax.experimental import pallas as pl
from jax.experimental.pallas import tpu as pltpu
from jax.sharding import PartitionSpec as P

BLK = 128
PIECES = 2
NEG_FILL = -1e30
MESH = pl.DeviceIdType.MESH
F32 = jnp.float32
BF16 = jnp.bfloat16


def kernel(
    sizes,
    q_ref,
    k_ref,
    v_ref,
    scale_ref,
    ft_ref,
    fo_ref,
    fb_ref,
    ig_ref,
    fg_ref,
    out_ref,
    qd,
    kd,
    vd,
    wk,
    num,
    lifted,
    up_buf,
    tot_buf,
    r_buf,
    rs_buf,
    bcol,
    wcol,
    brow,
    grow,
    peak_l,
    den_l,
    fin,
    own_h,
    up_h,
    tot_h,
    r_h,
    rs_h,
    wts,
    up_s,
    up_r,
    dn_s,
    r_r,
    cx_s,
    hs,
):
    heads, dk, dv, nc, nz = sizes
    rows = q_ref.shape[0]
    pw = dv // PIECES
    pieces = heads * PIECES
    factor = 1.0 / math.sqrt(dk)
    g, c, z = lax.axis_index("grp"), lax.axis_index("ctx"), lax.axis_index("head")
    last = nz - 1
    has_up, has_down = z < last, z > 0
    at_end = z == last
    gives_row, has_row = at_end & (c < nc - 1), c > 0
    above = (g, c, jnp.minimum(z + 1, last))
    below = (g, c, jnp.maximum(z - 1, 0))
    after = (g, jnp.minimum(c + 1, nc - 1), z)
    earlier = (g, jnp.maximum(c - 1, 0), z)

    barrier = pltpu.get_barrier_semaphore()
    greet = ((has_up, above), (has_down, below), (gives_row, after), (at_end & has_row, earlier))
    for there, who in greet:

        @pl.when(there)
        def _(who=who):
            pl.semaphore_signal(barrier, inc=1, device_id=who, device_id_type=MESH)

    def remote(src, dst, ssem, rsem, who):
        return pltpu.make_async_remote_copy(
            src_ref=src, dst_ref=dst, send_sem=ssem, recv_sem=rsem,
            device_id=who, device_id_type=MESH,
        )

    def up_copy(i):
        return remote(tot_buf.at[i], up_buf.at[i], up_s.at[i], up_r.at[i], above)

    def down_copy(i):
        return remote(r_buf.at[i], r_buf.at[i], dn_s.at[i], r_r.at[i], below)

    def row_copy(i):
        return remote(rs_buf.at[i], r_buf.at[i], cx_s.at[i], r_r.at[i], after)

    up_head = remote(tot_h, up_h, hs.at[0], hs.at[1], above)
    down_head = remote(r_h, r_h, hs.at[2], hs.at[3], below)
    row_head = remote(rs_h, r_h, hs.at[4], hs.at[3], after)

    token = lax.broadcasted_iota(jnp.int32, (BLK, 1), 0)

    def dequant(codes, e, h, width, kept):
        col = lax.broadcasted_iota(jnp.int32, (BLK, width), 1)
        start = pl.multiple_of(h * width, width)
        for b in range(rows // BLK):
            place = (pl.ds(b * BLK, BLK), pl.ds(start, width))
            off = fo_ref[b, h]
            bit = fb_ref[b, h]
            flip = jnp.where(bit >= 1, -2.0, -1.0)
            flip = flip * jnp.where(bit >= 2, 2.0, 1.0) * jnp.where(bit >= 3, 2.0, 1.0)
            flip = jnp.where(ft_ref[b, h] == e, flip, 1.0)
            hit = lax.rem(lax.rem(off, dv), width)
            line = jnp.where(token == lax.div(off, dv), hit, -1)
            scale = scale_ref[b, e, h]
            times = jnp.where(col == line, scale * flip, scale)
            kept[place] = (codes[place].astype(F32) * times).astype(BF16)
        return start

    lane = lax.broadcasted_iota(jnp.int32, (rows, heads), 1)

    def column(ref, h):
        return jnp.sum(jnp.where(lane == h, ref[...], 0.0), axis=1, keepdims=True)

    line_t = lax.broadcasted_iota(jnp.int32, (rows, rows), 0)
    line_s = lax.broadcasted_iota(jnp.int32, (rows, rows), 1)
    forget = fg_ref[...].astype(F32)
    logf = -(jnp.maximum(-forget, 0.0) + jnp.log1p(jnp.exp(-jnp.abs(forget))))
    gate = ig_ref[...].astype(F32)
    running = jnp.dot(
        (line_t >= line_s).astype(F32), logf,
        preferred_element_type=F32, precision=lax.Precision.HIGHEST,
    )
    bcol[...] = running
    brow[...] = running.T
    grow[...] = gate.T
    exponent = running[rows - 1 : rows, :] - running + gate
    wcol[...] = jnp.exp(exponent - jnp.max(exponent, axis=0, keepdims=True))
    total = brow[:, rows - 1 : rows]
    peak = jnp.max(total - brow[...] + grow[...], axis=1, keepdims=True)
    own_h[:, dk : 2 * dk] = jnp.broadcast_to(peak, (heads, dk))
    own_h[:, 2 * dk :] = jnp.broadcast_to(total, (heads, dk))

    def keys(h, carry):
        start = dequant(k_ref, 1, h, dk, kd)
        place = (slice(None), pl.ds(start, dk))
        weighted = (kd[place].astype(F32) * column(wcol, h)).astype(BF16)
        wk[place] = weighted
        own_h[pl.ds(h, 1), pl.ds(0, dk)] = jnp.sum(weighted.astype(F32), axis=0, keepdims=True)
        return carry

    lax.fori_loop(0, heads, keys, 0)

    def empty_header(ref):
        ref[:, 0:dk] = jnp.zeros((heads, dk), F32)
        ref[:, dk : 2 * dk] = jnp.full((heads, dk), NEG_FILL, F32)
        ref[:, 2 * dk :] = jnp.zeros((heads, dk), F32)

    @pl.when(z == 0)
    def _():
        empty_header(up_h)
        up_buf[...] = jnp.zeros_like(up_buf)

    @pl.when(c == 0)
    def _():
        empty_header(r_h)
        r_buf[...] = jnp.zeros_like(r_buf)

    def join(first, later, dst, at):
        m1, m2, f2 = first[:, dk : 2 * dk], later[:, dk : 2 * dk], later[:, 2 * dk :]
        m = jnp.maximum(m1 + f2, m2)
        w1, w2 = jnp.exp(m1 + f2 - m), jnp.exp(m2 - m)
        wts[at] = w1
        wts[at + 1] = w2
        dst[:, 0:dk] = w1 * first[:, 0:dk] + w2 * later[:, 0:dk]
        dst[:, dk : 2 * dk] = m
        dst[:, 2 * dk :] = first[:, 2 * dk :] + f2

    greeted = sum(there.astype(jnp.int32) for there, _ in greet)
    pl.semaphore_wait(barrier, greeted)

    @pl.when(has_down)
    def _():
        up_head.wait_recv()

    join(up_h, own_h, tot_h, 0)

    @pl.when(has_up)
    def _():
        up_head.start()

    def weight(at, h):
        return wts[at, pl.ds(h, 1), :][:, 0:pw]

    def local(h):
        start = dequant(q_ref, 0, h, dk, qd)
        place = (slice(None), pl.ds(start, dk))
        scores = lax.dot_general(
            qd[place], kd[place], (((1,), (1,)), ((), ())), preferred_element_type=F32
        ) * factor
        gaps = column(bcol, h) - brow[pl.ds(h, 1), :] + grow[pl.ds(h, 1), :]
        gaps = jnp.where(line_t >= line_s, gaps, NEG_FILL)
        top = jnp.max(gaps, axis=1, keepdims=True)
        product = jnp.exp(gaps - top) * scores
        peak_l[h] = jnp.broadcast_to(top, (rows, BLK))
        den_l[h] = jnp.broadcast_to(jnp.sum(product, axis=1, keepdims=True), (rows, BLK))
        wide = (slice(None), pl.ds(pl.multiple_of(h * dv, dv), dv))
        num[wide] = jnp.dot(product.astype(BF16), vd[wide], preferred_element_type=F32)

    def upward(i):
        h = lax.div(i, PIECES)

        @pl.when(lax.rem(i, PIECES) == 0)
        def _():
            dequant(v_ref, 2, h, dv, vd)

        piece = pl.ds(pl.multiple_of(i * pw, pw), pw)
        state = lax.dot_general(
            wk[:, pl.ds(pl.multiple_of(h * dk, dk), dk)], vd[:, piece],
            (((0,), (0,)), ((), ())), preferred_element_type=F32,
        )

        @pl.when(has_down)
        def _():
            up_copy(i).wait_recv()

        tot_buf[i] = (weight(0, h) * up_buf[i].astype(F32) + weight(1, h) * state).astype(BF16)

        @pl.when(has_up)
        def _():
            up_copy(i).start()

        @pl.when(lax.rem(i, PIECES) == 0)
        def _():
            local(h)

    def header_row():
        @pl.when(has_row)
        def _():
            down_head.wait_recv()

        @pl.when(has_row & has_down)
        def _():
            down_head.start()

        @pl.when(gives_row)
        def _():
            join(r_h, tot_h, rs_h, 2)
            row_head.start()

        join(r_h, up_h, own_h, 4)

    def finish(j):
        h = lax.div(j, PIECES)

        @pl.when(j == 0)
        def _():
            header_row()

        @pl.when(has_row)
        def _():
            down_copy(j).wait_recv()

        @pl.when(has_row & has_down)
        def _():
            down_copy(j).start()

        arrived = r_buf[j].astype(F32)

        @pl.when(gives_row)
        def _():
            rs_buf[j] = (weight(2, h) * arrived + weight(3, h) * tot_buf[j].astype(F32)).astype(BF16)
            row_copy(j).start()

        @pl.when(lax.rem(j, PIECES) == 0)
        def _():
            place = (slice(None), pl.ds(pl.multiple_of(h * dk, dk), dk))
            header = own_h[pl.ds(h, 1), :]
            norm, m = header[:, 0:dk], header[:, dk : dk + BLK]
            inter = column(bcol, h) + m
            top = jnp.maximum(peak_l[h], inter)
            shrink = jnp.exp(peak_l[h] - top)
            lift = jnp.exp(inter - top) * factor
            raised = (qd[place].astype(F32) * lift[:, 0:1]).astype(BF16)
            lifted[...] = raised
            den = shrink * den_l[h] + jnp.sum(raised.astype(F32) * norm, axis=1, keepdims=True)
            fin[0] = shrink
            fin[1] = 1.0 / jnp.maximum(jnp.abs(den), 1.0)

        piece = pl.ds(pl.multiple_of(j * pw, pw), pw)
        begin = (weight(4, h) * arrived + weight(5, h) * up_buf[j].astype(F32)).astype(BF16)
        above_line = num[:, piece] * fin[0][:, 0:1] + jnp.dot(
            lifted[...], begin, preferred_element_type=F32
        )
        out_ref[:, piece] = (above_line * fin[1][:, 0:1]).astype(BF16)

    skew = 2 * (last - z) + c

    def step(t, carry):
        @pl.when(t < pieces)
        def _():
            upward(t)

        @pl.when(t >= skew)
        def _():
            finish(t - skew)

        return carry

    lax.fori_loop(0, pieces + skew, step, 0)

    @pl.when(has_up)
    def _():
        up_head.wait_send()

    @pl.when(has_row & has_down)
    def _():
        down_head.wait_send()

    @pl.when(gives_row)
    def _():
        row_head.wait_send()

    def drain(i, carry):
        @pl.when(has_up)
        def _():
            up_copy(i).wait_send()

        @pl.when(has_row & has_down)
        def _():
            down_copy(i).wait_send()

        @pl.when(gives_row)
        def _():
            row_copy(i).wait_send()

        return carry

    lax.fori_loop(0, pieces, drain, 0)


def body(nc, nz, *args):
    rows = args[0].shape[0]
    heads = args[3].shape[2]
    dk, dv = args[0].shape[1] // heads, args[2].shape[1] // heads
    pieces, pw = heads * PIECES, dv // PIECES
    vmem, smem = pl.BlockSpec(memory_space=pltpu.VMEM), pl.BlockSpec(memory_space=pltpu.SMEM)
    passed = pltpu.VMEM((pieces, dk, pw), BF16)
    header = pltpu.VMEM((heads, 3 * dk), F32)
    sems = pltpu.SemaphoreType.DMA((pieces,))
    return pl.pallas_call(
        functools.partial(kernel, (heads, dk, dv, nc, nz)),
        out_shape=jax.ShapeDtypeStruct((rows, heads * dv), BF16),
        in_specs=[vmem] * 3 + [smem] * 4 + [vmem] * 2,
        out_specs=vmem,
        scratch_shapes=[
            pltpu.VMEM((rows, heads * dk), BF16),
            pltpu.VMEM((rows, heads * dk), BF16),
            pltpu.VMEM((rows, heads * dv), BF16),
            pltpu.VMEM((rows, heads * dk), BF16),
            pltpu.VMEM((rows, heads * dv), F32),
            pltpu.VMEM((rows, dk), BF16),
            passed,
            passed,
            passed,
            passed,
            pltpu.VMEM((rows, heads), F32),
            pltpu.VMEM((rows, heads), F32),
            pltpu.VMEM((heads, rows), F32),
            pltpu.VMEM((heads, rows), F32),
            pltpu.VMEM((heads, rows, BLK), F32),
            pltpu.VMEM((heads, rows, BLK), F32),
            pltpu.VMEM((2, rows, BLK), F32),
            header,
            header,
            header,
            header,
            header,
            pltpu.VMEM((6, heads, dk), F32),
            sems,
            sems,
            sems,
            sems,
            sems,
            pltpu.SemaphoreType.DMA((5,)),
        ],
        compiler_params=pltpu.CompilerParams(
            collective_id=0, has_side_effects=True, vmem_limit_bytes=48 * 1024 * 1024
        ),
    )(*args)


def solution(mesh):
    rows = ("grp", "ctx", "head")
    placed = tuple(P(rows, *([None] * (n - 1))) for n in (2, 2, 2, 3, 2, 2, 2, 2, 2))
    return jax.shard_map(
        functools.partial(body, mesh.shape["ctx"], mesh.shape["head"]),
        mesh=mesh, in_specs=placed, out_specs=P(rows, None), check_vma=False,
    )
```

```python
import functools
import math

import jax
import jax.numpy as jnp
from jax import lax
from jax.experimental import pallas as pl
from jax.experimental.pallas import tpu as pltpu
from jax.sharding import PartitionSpec as P

BLK = 128
PIECES = 4
Z_SKEW = 6
C_SKEW = 3
NEG_FILL = -1e30
MESH = pl.DeviceIdType.MESH
F32 = jnp.float32
BF16 = jnp.bfloat16


def kernel(
    sizes,
    q_ref,
    k_ref,
    v_ref,
    scale_ref,
    ft_ref,
    fo_ref,
    fb_ref,
    ig_ref,
    fg_ref,
    out_ref,
    qd,
    kd,
    vd,
    wk,
    num,
    state,
    lifted,
    up_buf,
    tot_buf,
    r_buf,
    rs_buf,
    bcol,
    wcol,
    brow,
    grow,
    peak_l,
    den_l,
    fin,
    own_h,
    up_h,
    tot_h,
    r_h,
    rs_h,
    wts,
    up_s,
    up_r,
    dn_s,
    r_r,
    cx_s,
    hs,
):
    heads, dk, dv, nc, nz = sizes
    rows = q_ref.shape[0]
    pw = dv // PIECES
    pieces = heads * PIECES
    factor = 1.0 / math.sqrt(dk)
    g, c, z = lax.axis_index("grp"), lax.axis_index("ctx"), lax.axis_index("head")
    last = nz - 1
    has_up, has_down = z < last, z > 0
    at_end = z == last
    gives_row, has_row = at_end & (c < nc - 1), c > 0
    above = (g, c, jnp.minimum(z + 1, last))
    below = (g, c, jnp.maximum(z - 1, 0))
    after = (g, jnp.minimum(c + 1, nc - 1), z)
    earlier = (g, jnp.maximum(c - 1, 0), z)

    barrier = pltpu.get_barrier_semaphore()
    greet = ((has_up, above), (has_down, below), (gives_row, after), (at_end & has_row, earlier))
    for there, who in greet:

        @pl.when(there)
        def _(who=who):
            pl.semaphore_signal(barrier, inc=1, device_id=who, device_id_type=MESH)

    def remote(src, dst, ssem, rsem, who):
        return pltpu.make_async_remote_copy(
            src_ref=src, dst_ref=dst, send_sem=ssem, recv_sem=rsem,
            device_id=who, device_id_type=MESH,
        )

    def up_copy(i):
        return remote(tot_buf.at[i], up_buf.at[i], up_s.at[i], up_r.at[i], above)

    def down_copy(i):
        return remote(r_buf.at[i], r_buf.at[i], dn_s.at[i], r_r.at[i], below)

    def row_copy(i):
        return remote(rs_buf.at[i], r_buf.at[i], cx_s.at[i], r_r.at[i], after)

    up_head = remote(tot_h, up_h, hs.at[0], hs.at[1], above)
    down_head = remote(r_h, r_h, hs.at[2], hs.at[3], below)
    row_head = remote(rs_h, r_h, hs.at[4], hs.at[3], after)

    token = lax.broadcasted_iota(jnp.int32, (BLK, 1), 0)

    def dequant(codes, e, h, width, kept):
        col = lax.broadcasted_iota(jnp.int32, (BLK, width), 1)
        start = pl.multiple_of(h * width, width)
        for b in range(rows // BLK):
            place = (pl.ds(b * BLK, BLK), pl.ds(start, width))
            off = fo_ref[b, h]
            bit = fb_ref[b, h]
            flip = jnp.where(bit >= 1, -2.0, -1.0)
            flip = flip * jnp.where(bit >= 2, 2.0, 1.0) * jnp.where(bit >= 3, 2.0, 1.0)
            flip = jnp.where(ft_ref[b, h] == e, flip, 1.0)
            hit = lax.rem(lax.rem(off, dv), width)
            line = jnp.where(token == lax.div(off, dv), hit, -1)
            scale = scale_ref[b, e, h]
            times = jnp.where(col == line, scale * flip, scale)
            kept[place] = (codes[place].astype(F32) * times).astype(BF16)
        return start

    lane = lax.broadcasted_iota(jnp.int32, (rows, heads), 1)

    def column(ref, h):
        return jnp.sum(jnp.where(lane == h, ref[...], 0.0), axis=1, keepdims=True)

    line_t = lax.broadcasted_iota(jnp.int32, (rows, rows), 0)
    line_s = lax.broadcasted_iota(jnp.int32, (rows, rows), 1)
    forget = fg_ref[...].astype(F32)
    logf = -(jnp.maximum(-forget, 0.0) + jnp.log1p(jnp.exp(-jnp.abs(forget))))
    gate = ig_ref[...].astype(F32)
    running = jnp.dot(
        (line_t >= line_s).astype(F32), logf,
        preferred_element_type=F32, precision=lax.Precision.HIGHEST,
    )
    bcol[...] = running
    brow[...] = running.T
    grow[...] = gate.T
    exponent = running[rows - 1 : rows, :] - running + gate
    wcol[...] = jnp.exp(exponent - jnp.max(exponent, axis=0, keepdims=True))
    total = brow[:, rows - 1 : rows]
    peak = jnp.max(total - brow[...] + grow[...], axis=1, keepdims=True)
    own_h[:, dk : 2 * dk] = jnp.broadcast_to(peak, (heads, dk))
    own_h[:, 2 * dk :] = jnp.broadcast_to(total, (heads, dk))

    def keys(h, carry):
        start = dequant(k_ref, 1, h, dk, kd)
        place = (slice(None), pl.ds(start, dk))
        weighted = (kd[place].astype(F32) * column(wcol, h)).astype(BF16)
        wk[place] = weighted
        own_h[pl.ds(h, 1), pl.ds(0, dk)] = jnp.sum(weighted.astype(F32), axis=0, keepdims=True)
        return carry

    lax.fori_loop(0, heads, keys, 0)

    def empty_header(ref):
        ref[:, 0:dk] = jnp.zeros((heads, dk), F32)
        ref[:, dk : 2 * dk] = jnp.full((heads, dk), NEG_FILL, F32)
        ref[:, 2 * dk :] = jnp.zeros((heads, dk), F32)

    @pl.when(z == 0)
    def _():
        empty_header(up_h)
        up_buf[...] = jnp.zeros_like(up_buf)

    @pl.when(c == 0)
    def _():
        empty_header(r_h)
        r_buf[...] = jnp.zeros_like(r_buf)

    def join(first, later, dst, at):
        m1, m2, f2 = first[:, dk : 2 * dk], later[:, dk : 2 * dk], later[:, 2 * dk :]
        m = jnp.maximum(m1 + f2, m2)
        w1, w2 = jnp.exp(m1 + f2 - m), jnp.exp(m2 - m)
        wts[at] = w1
        wts[at + 1] = w2
        dst[:, 0:dk] = w1 * first[:, 0:dk] + w2 * later[:, 0:dk]
        dst[:, dk : 2 * dk] = m
        dst[:, 2 * dk :] = first[:, 2 * dk :] + f2

    greeted = sum(there.astype(jnp.int32) for there, _ in greet)
    pl.semaphore_wait(barrier, greeted)

    @pl.when(has_down)
    def _():
        up_head.wait_recv()

    join(up_h, own_h, tot_h, 0)

    @pl.when(has_up)
    def _():
        up_head.start()

    def weight(at, h):
        return wts[at, pl.ds(h, 1), :][:, 0:pw]

    def local(h):
        start = dequant(q_ref, 0, h, dk, qd)
        place = (slice(None), pl.ds(start, dk))
        scores = lax.dot_general(
            qd[place], kd[place], (((1,), (1,)), ((), ())), preferred_element_type=F32
        ) * factor
        gaps = column(bcol, h) - brow[pl.ds(h, 1), :] + grow[pl.ds(h, 1), :]
        gaps = jnp.where(line_t >= line_s, gaps, NEG_FILL)
        top = jnp.max(gaps, axis=1, keepdims=True)
        product = jnp.exp(gaps - top) * scores
        peak_l[h] = jnp.broadcast_to(top, (rows, BLK))
        den_l[h] = jnp.broadcast_to(jnp.sum(product, axis=1, keepdims=True), (rows, BLK))
        wide = (slice(None), pl.ds(pl.multiple_of(h * dv, dv), dv))
        num[wide] = jnp.dot(product.astype(BF16), vd[wide], preferred_element_type=F32)

    def head_state(h):
        wide = (slice(None), pl.ds(pl.multiple_of(h * dv, dv), dv))
        found = lax.dot_general(
            wk[:, pl.ds(pl.multiple_of(h * dk, dk), dk)], vd[wide],
            (((0,), (0,)), ((), ())), preferred_element_type=F32,
        )
        for p in range(PIECES):
            state[p] = found[:, p * pw : (p + 1) * pw]

    def upward(i):
        h = lax.div(i, PIECES)

        @pl.when(has_down)
        def _():
            up_copy(i).wait_recv()

        mine = state[lax.rem(i, PIECES)]
        tot_buf[i] = (weight(0, h) * up_buf[i].astype(F32) + weight(1, h) * mine).astype(BF16)

        @pl.when(has_up)
        def _():
            up_copy(i).start()

    def ahead(i):
        h, p = lax.div(i, PIECES), lax.rem(i, PIECES)

        @pl.when(p == 0)
        def _():
            local(h)

        @pl.when((p == PIECES - 2) & (h + 1 < heads))
        def _():
            dequant(v_ref, 2, h + 1, dv, vd)

        @pl.when((p == PIECES - 1) & (h + 1 < heads))
        def _():
            head_state(h + 1)

    def header_row():
        @pl.when(has_row)
        def _():
            down_head.wait_recv()

        @pl.when(has_row & has_down)
        def _():
            down_head.start()

        @pl.when(gives_row)
        def _():
            join(r_h, tot_h, rs_h, 2)
            row_head.start()

        join(r_h, up_h, own_h, 4)

    def forward(j):
        h = lax.div(j, PIECES)

        @pl.when(j == 0)
        def _():
            header_row()

        @pl.when(has_row)
        def _():
            down_copy(j).wait_recv()

        @pl.when(has_row & has_down)
        def _():
            down_copy(j).start()

        @pl.when(gives_row)
        def _():
            rs_buf[j] = (
                weight(2, h) * r_buf[j].astype(F32) + weight(3, h) * tot_buf[j].astype(F32)
            ).astype(BF16)
            row_copy(j).start()

    def finish(j):
        h = lax.div(j, PIECES)

        @pl.when(lax.rem(j, PIECES) == 0)
        def _():
            place = (slice(None), pl.ds(pl.multiple_of(h * dk, dk), dk))
            header = own_h[pl.ds(h, 1), :]
            norm, m = header[:, 0:dk], header[:, dk : dk + BLK]
            inter = column(bcol, h) + m
            top = jnp.maximum(peak_l[h], inter)
            shrink = jnp.exp(peak_l[h] - top)
            lift = jnp.exp(inter - top) * factor
            raised = (qd[place].astype(F32) * lift[:, 0:1]).astype(BF16)
            lifted[...] = raised
            den = shrink * den_l[h] + jnp.sum(raised.astype(F32) * norm, axis=1, keepdims=True)
            fin[0] = shrink
            fin[1] = 1.0 / jnp.maximum(jnp.abs(den), 1.0)

        piece = pl.ds(pl.multiple_of(j * pw, pw), pw)
        begin = (weight(4, h) * r_buf[j].astype(F32) + weight(5, h) * up_buf[j].astype(F32)).astype(BF16)
        above_line = num[:, piece] * fin[0][:, 0:1] + jnp.dot(
            lifted[...], begin, preferred_element_type=F32
        )
        out_ref[:, piece] = (above_line * fin[1][:, 0:1]).astype(BF16)

    skew = Z_SKEW * (last - z) + C_SKEW * c
    dequant(v_ref, 2, 0, dv, vd)
    head_state(0)

    def step(t, carry):
        @pl.when(t < pieces)
        def _():
            upward(t)

        @pl.when(t >= skew)
        def _():
            forward(t - skew)

        @pl.when(t < pieces)
        def _():
            ahead(t)

        @pl.when(t >= skew)
        def _():
            finish(t - skew)

        return carry

    lax.fori_loop(0, pieces + skew, step, 0)

    @pl.when(has_up)
    def _():
        up_head.wait_send()

    @pl.when(has_row & has_down)
    def _():
        down_head.wait_send()

    @pl.when(gives_row)
    def _():
        row_head.wait_send()

    def drain(i, carry):
        @pl.when(has_up)
        def _():
            up_copy(i).wait_send()

        @pl.when(has_row & has_down)
        def _():
            down_copy(i).wait_send()

        @pl.when(gives_row)
        def _():
            row_copy(i).wait_send()

        return carry

    lax.fori_loop(0, pieces, drain, 0)


def body(nc, nz, *args):
    rows = args[0].shape[0]
    heads = args[3].shape[2]
    dk, dv = args[0].shape[1] // heads, args[2].shape[1] // heads
    pieces, pw = heads * PIECES, dv // PIECES
    vmem, smem = pl.BlockSpec(memory_space=pltpu.VMEM), pl.BlockSpec(memory_space=pltpu.SMEM)
    passed = pltpu.VMEM((pieces, dk, pw), BF16)
    header = pltpu.VMEM((heads, 3 * dk), F32)
    sems = pltpu.SemaphoreType.DMA((pieces,))
    return pl.pallas_call(
        functools.partial(kernel, (heads, dk, dv, nc, nz)),
        out_shape=jax.ShapeDtypeStruct((rows, heads * dv), BF16),
        in_specs=[vmem] * 3 + [smem] * 4 + [vmem] * 2,
        out_specs=vmem,
        scratch_shapes=[
            pltpu.VMEM((rows, heads * dk), BF16),
            pltpu.VMEM((rows, heads * dk), BF16),
            pltpu.VMEM((rows, heads * dv), BF16),
            pltpu.VMEM((rows, heads * dk), BF16),
            pltpu.VMEM((rows, heads * dv), F32),
            pltpu.VMEM((PIECES, dk, pw), F32),
            pltpu.VMEM((rows, dk), BF16),
            passed,
            passed,
            passed,
            passed,
            pltpu.VMEM((rows, heads), F32),
            pltpu.VMEM((rows, heads), F32),
            pltpu.VMEM((heads, rows), F32),
            pltpu.VMEM((heads, rows), F32),
            pltpu.VMEM((heads, rows, BLK), F32),
            pltpu.VMEM((heads, rows, BLK), F32),
            pltpu.VMEM((2, rows, BLK), F32),
            header,
            header,
            header,
            header,
            header,
            pltpu.VMEM((6, heads, dk), F32),
            sems,
            sems,
            sems,
            sems,
            sems,
            pltpu.SemaphoreType.DMA((5,)),
        ],
        compiler_params=pltpu.CompilerParams(
            collective_id=0, has_side_effects=True, vmem_limit_bytes=48 * 1024 * 1024
        ),
    )(*args)


def solution(mesh):
    rows = ("grp", "ctx", "head")
    placed = tuple(P(rows, *([None] * (n - 1))) for n in (2, 2, 2, 3, 2, 2, 2, 2, 2))
    return jax.shard_map(
        functools.partial(body, mesh.shape["ctx"], mesh.shape["head"]),
        mesh=mesh, in_specs=placed, out_specs=P(rows, None), check_vma=False,
    )
```

```python
import functools
import math

import jax
import jax.numpy as jnp
from jax import lax
from jax.experimental import pallas as pl
from jax.experimental.pallas import tpu as pltpu
from jax.sharding import PartitionSpec as P

BLK = 128
PIECES = 4
Z_SKEW = 3
C_SKEW = 2
NEG_FILL = -1e30
MESH = pl.DeviceIdType.MESH
F32 = jnp.float32
BF16 = jnp.bfloat16


def kernel(
    sizes,
    q_any,
    k_any,
    v_any,
    scale_ref,
    ft_ref,
    fo_ref,
    fb_ref,
    ig_ref,
    fg_ref,
    out_any,
    out_ref,
    out_s,
    q_ref,
    k_ref,
    v_ref,
    in_s,
    qd,
    kd,
    vd,
    wk,
    num,
    state,
    lifted,
    inner,
    up_buf,
    tot_buf,
    r_buf,
    rs_buf,
    bcol,
    wcol,
    brow,
    grow,
    peak_l,
    den_l,
    fin,
    own_h,
    up_h,
    tot_h,
    r_h,
    rs_h,
    wts,
    up_s,
    up_r,
    dn_s,
    r_r,
    cx_s,
    hs,
):
    heads, dk, dv, nc, nz = sizes
    rows = q_ref.shape[0]
    k_in = pltpu.make_async_copy(k_any, k_ref, in_s.at[0])
    v_in = pltpu.make_async_copy(v_any, v_ref, in_s.at[1])
    q_in = pltpu.make_async_copy(q_any, q_ref, in_s.at[2])
    k_in.start()
    v_in.start()
    q_in.start()
    pw = dv // PIECES
    pieces = heads * PIECES
    factor = 1.0 / math.sqrt(dk)
    g, c, z = lax.axis_index("grp"), lax.axis_index("ctx"), lax.axis_index("head")
    last = nz - 1
    has_up, has_down = z < last, z > 0
    at_end = z == last
    gives_row, has_row = at_end & (c < nc - 1), c > 0
    above = (g, c, jnp.minimum(z + 1, last))
    below = (g, c, jnp.maximum(z - 1, 0))
    after = (g, jnp.minimum(c + 1, nc - 1), z)
    earlier = (g, jnp.maximum(c - 1, 0), z)

    barrier = pltpu.get_barrier_semaphore()
    greet = ((has_up, above), (has_down, below), (gives_row, after), (at_end & has_row, earlier))
    for there, who in greet:

        @pl.when(there)
        def _(who=who):
            pl.semaphore_signal(barrier, inc=1, device_id=who, device_id_type=MESH)

    def remote(src, dst, ssem, rsem, who):
        return pltpu.make_async_remote_copy(
            src_ref=src, dst_ref=dst, send_sem=ssem, recv_sem=rsem,
            device_id=who, device_id_type=MESH,
        )

    def up_copy(i):
        return remote(tot_buf.at[i], up_buf.at[i], up_s.at[i], up_r.at[i], above)

    def down_copy(i):
        return remote(r_buf.at[i], r_buf.at[i], dn_s.at[i], r_r.at[i], below)

    def row_copy(i):
        return remote(rs_buf.at[i], r_buf.at[i], cx_s.at[i], r_r.at[i], after)

    up_head = remote(tot_h, up_h, hs.at[0], hs.at[1], above)
    down_head = remote(r_h, r_h, hs.at[2], hs.at[3], below)
    row_head = remote(rs_h, r_h, hs.at[4], hs.at[3], after)

    token = lax.broadcasted_iota(jnp.int32, (BLK, 1), 0)

    def dequant(codes, e, h, width, kept):
        col = lax.broadcasted_iota(jnp.int32, (BLK, width), 1)
        start = pl.multiple_of(h * width, width)
        for b in range(rows // BLK):
            place = (pl.ds(b * BLK, BLK), pl.ds(start, width))
            off = fo_ref[b, h]
            bit = fb_ref[b, h]
            flip = jnp.where(bit >= 1, -2.0, -1.0)
            flip = flip * jnp.where(bit >= 2, 2.0, 1.0) * jnp.where(bit >= 3, 2.0, 1.0)
            flip = jnp.where(ft_ref[b, h] == e, flip, 1.0)
            hit = lax.rem(lax.rem(off, dv), width)
            line = jnp.where(token == lax.div(off, dv), hit, -1)
            scale = scale_ref[e, b, h]
            times = jnp.where(col == line, scale * flip, scale)
            kept[place] = (codes[place].astype(F32) * times).astype(BF16)
        return start

    lane = lax.broadcasted_iota(jnp.int32, (rows, heads), 1)

    def column(ref, h):
        return jnp.sum(jnp.where(lane == h, ref[...], 0.0), axis=1, keepdims=True)

    line_t = lax.broadcasted_iota(jnp.int32, (rows, rows), 0)
    line_s = lax.broadcasted_iota(jnp.int32, (rows, rows), 1)
    forget = fg_ref[...].astype(F32)
    logf = -(jnp.maximum(-forget, 0.0) + jnp.log1p(jnp.exp(-jnp.abs(forget))))
    gate = ig_ref[...].astype(F32)
    running = jnp.dot(
        logf, (line_t <= line_s).astype(F32),
        preferred_element_type=F32, precision=lax.Precision.HIGHEST,
    )
    brow[...] = running
    bcol[...] = running.T
    grow[...] = gate
    total = running[:, rows - 1 : rows]
    exponent = total - running + gate
    peak = jnp.max(exponent, axis=1, keepdims=True)
    wcol[...] = jnp.exp(exponent - peak).T
    own_h[:, dk : 2 * dk] = jnp.broadcast_to(peak, (heads, dk))
    own_h[:, 2 * dk :] = jnp.broadcast_to(total, (heads, dk))

    k_in.wait()

    def keys(h, carry):
        start = dequant(k_ref, 1, h, dk, kd)
        place = (slice(None), pl.ds(start, dk))
        weighted = (kd[place].astype(F32) * column(wcol, h)).astype(BF16)
        wk[place] = weighted
        own_h[pl.ds(h, 1), pl.ds(0, dk)] = jnp.sum(weighted.astype(F32), axis=0, keepdims=True)
        return carry

    lax.fori_loop(0, heads, keys, 0, unroll=2)

    def empty_header(ref):
        ref[:, 0:dk] = jnp.zeros((heads, dk), F32)
        ref[:, dk : 2 * dk] = jnp.full((heads, dk), NEG_FILL, F32)
        ref[:, 2 * dk :] = jnp.zeros((heads, dk), F32)

    @pl.when(z == 0)
    def _():
        empty_header(up_h)
        up_buf[...] = jnp.zeros_like(up_buf)

    @pl.when(c == 0)
    def _():
        empty_header(r_h)
        r_buf[...] = jnp.zeros_like(r_buf)

    def join(first, later, dst, at):
        m1, m2, f2 = first[:, dk : 2 * dk], later[:, dk : 2 * dk], later[:, 2 * dk :]
        m = jnp.maximum(m1 + f2, m2)
        w1, w2 = jnp.exp(m1 + f2 - m), jnp.exp(m2 - m)
        wts[at] = w1
        wts[at + 1] = w2
        dst[:, 0:dk] = w1 * first[:, 0:dk] + w2 * later[:, 0:dk]
        dst[:, dk : 2 * dk] = m
        dst[:, 2 * dk :] = first[:, 2 * dk :] + f2

    greeted = sum(there.astype(jnp.int32) for there, _ in greet)
    pl.semaphore_wait(barrier, greeted)

    @pl.when(has_down)
    def _():
        up_head.wait_recv()

    join(up_h, own_h, tot_h, 0)

    @pl.when(has_up)
    def _():
        up_head.start()

    def weight(at, h):
        return wts[at, pl.ds(h, 1), :][:, 0:pw]

    def local(h):
        start = dequant(q_ref, 0, h, dk, qd)
        place = (slice(None), pl.ds(start, dk))
        scores = lax.dot_general(
            qd[place], kd[place], (((1,), (1,)), ((), ())), preferred_element_type=F32
        ) * factor
        gaps = column(bcol, h) - brow[pl.ds(h, 1), :] + grow[pl.ds(h, 1), :]
        gaps = jnp.where(line_t >= line_s, gaps, NEG_FILL)
        top = jnp.max(gaps, axis=1, keepdims=True)
        product = jnp.exp(gaps - top) * scores
        peak_l[h] = jnp.broadcast_to(top, (rows, BLK))
        den_l[h] = jnp.broadcast_to(jnp.sum(product, axis=1, keepdims=True), (rows, BLK))
        inner[...] = product.astype(BF16)

    def local_values(h):
        wide = (slice(None), pl.ds(pl.multiple_of(h * dv, dv), dv))
        num[wide] = jnp.dot(inner[...], vd[wide], preferred_element_type=F32)

    def head_state(h):
        wide = (slice(None), pl.ds(pl.multiple_of(h * dv, dv), dv))
        found = lax.dot_general(
            wk[:, pl.ds(pl.multiple_of(h * dk, dk), dk)], vd[wide],
            (((0,), (0,)), ((), ())), preferred_element_type=F32,
        )
        for p in range(PIECES):
            state[p] = found[:, p * pw : (p + 1) * pw]

    def upward(i):
        h = lax.div(i, PIECES)

        @pl.when(has_down)
        def _():
            up_copy(i).wait_recv()

        mine = state[lax.rem(i, PIECES)]
        tot_buf[i] = (weight(0, h) * up_buf[i].astype(F32) + weight(1, h) * mine).astype(BF16)

        @pl.when(has_up)
        def _():
            up_copy(i).start()

    def ahead(i):
        h, p = lax.div(i, PIECES), lax.rem(i, PIECES)

        @pl.when(p == 0)
        def _():
            local(h)

        @pl.when(p == min(1, PIECES - 1))
        def _():
            local_values(h)

        @pl.when((p == PIECES - 2) & (h + 1 < heads))
        def _():
            dequant(v_ref, 2, h + 1, dv, vd)

        @pl.when((p == PIECES - 1) & (h + 1 < heads))
        def _():
            head_state(h + 1)

    def header_row():
        @pl.when(has_row)
        def _():
            down_head.wait_recv()

        @pl.when(has_row & has_down)
        def _():
            down_head.start()

        @pl.when(gives_row)
        def _():
            join(r_h, tot_h, rs_h, 2)
            row_head.start()

        join(r_h, up_h, own_h, 4)

    def forward(j):
        h = lax.div(j, PIECES)

        @pl.when(j == 0)
        def _():
            header_row()

        @pl.when(has_row)
        def _():
            down_copy(j).wait_recv()

        @pl.when(has_row & has_down)
        def _():
            down_copy(j).start()

        @pl.when(gives_row)
        def _():
            rs_buf[j] = (
                weight(2, h) * r_buf[j].astype(F32) + weight(3, h) * tot_buf[j].astype(F32)
            ).astype(BF16)
            row_copy(j).start()

    def finish(j):
        h = lax.div(j, PIECES)

        @pl.when(lax.rem(j, PIECES) == 0)
        def _():
            place = (slice(None), pl.ds(pl.multiple_of(h * dk, dk), dk))
            header = own_h[pl.ds(h, 1), :]
            norm, m = header[:, 0:dk], header[:, dk : dk + BLK]
            inter = column(bcol, h) + m
            top = jnp.maximum(peak_l[h], inter)
            shrink = jnp.exp(peak_l[h] - top)
            lift = jnp.exp(inter - top) * factor
            raised = (qd[place].astype(F32) * lift[:, 0:1]).astype(BF16)
            lifted[...] = raised
            den = shrink * den_l[h] + jnp.sum(raised.astype(F32) * norm, axis=1, keepdims=True)
            fin[0] = shrink
            fin[1] = 1.0 / jnp.maximum(jnp.abs(den), 1.0)

        piece = pl.ds(pl.multiple_of(j * pw, pw), pw)
        begin = (weight(4, h) * r_buf[j].astype(F32) + weight(5, h) * up_buf[j].astype(F32)).astype(BF16)
        above_line = num[:, piece] * fin[0][:, 0:1] + jnp.dot(
            lifted[...], begin, preferred_element_type=F32
        )
        out_ref[:, piece] = (above_line * fin[1][:, 0:1]).astype(BF16)

        @pl.when(lax.rem(j, PIECES) == PIECES - 1)
        def _():
            out_copy(h).start()

    def out_copy(h):
        wide = (slice(None), pl.ds(pl.multiple_of(h * dv, dv), dv))
        return pltpu.make_async_copy(out_ref.at[wide], out_any.at[wide], out_s.at[h])

    skew = Z_SKEW * (last - z) + C_SKEW * c
    v_in.wait()
    dequant(v_ref, 2, 0, dv, vd)
    head_state(0)
    q_in.wait()

    def step(t, carry):
        @pl.when(t < pieces)
        def _():
            upward(t)

        @pl.when((t >= skew) & (t < pieces + skew))
        def _():
            forward(t - skew)

        @pl.when(t < pieces)
        def _():
            ahead(t)

        @pl.when(t > skew)
        def _():
            finish(t - skew - 1)

        return carry

    lax.fori_loop(0, pieces + skew + 1, step, 0)

    @pl.when(has_up)
    def _():
        up_head.wait_send()

    @pl.when(has_row & has_down)
    def _():
        down_head.wait_send()

    @pl.when(gives_row)
    def _():
        row_head.wait_send()

    def drain_out(h, carry):
        out_copy(h).wait()
        return carry

    lax.fori_loop(0, heads, drain_out, 0)

    def drain(i, carry):
        @pl.when(has_up)
        def _():
            up_copy(i).wait_send()

        @pl.when(has_row & has_down)
        def _():
            down_copy(i).wait_send()

        @pl.when(gives_row)
        def _():
            row_copy(i).wait_send()

        return carry

    lax.fori_loop(0, pieces, drain, 0)


def body(nc, nz, *args):
    rows = args[0].shape[0]
    heads = args[3].shape[2]
    dk, dv = args[0].shape[1] // heads, args[2].shape[1] // heads
    pieces, pw = heads * PIECES, dv // PIECES
    vmem, smem = pl.BlockSpec(memory_space=pltpu.VMEM), pl.BlockSpec(memory_space=pltpu.SMEM)
    passed = pltpu.VMEM((pieces, dk, pw), BF16)
    header = pltpu.VMEM((heads, 3 * dk), F32)
    sems = pltpu.SemaphoreType.DMA((pieces,))
    return pl.pallas_call(
        functools.partial(kernel, (heads, dk, dv, nc, nz)),
        out_shape=jax.ShapeDtypeStruct((rows, heads * dv), BF16),
        in_specs=[pl.BlockSpec(memory_space=pl.ANY)] * 3 + [smem] * 4 + [vmem] * 2,
        out_specs=pl.BlockSpec(memory_space=pl.ANY),
        scratch_shapes=[
            pltpu.VMEM((rows, heads * dv), BF16),
            pltpu.SemaphoreType.DMA((heads,)),
            pltpu.VMEM((rows, heads * dk), BF16),
            pltpu.VMEM((rows, heads * dk), BF16),
            pltpu.VMEM((rows, heads * dv), BF16),
            pltpu.SemaphoreType.DMA((3,)),
            pltpu.VMEM((rows, heads * dk), BF16),
            pltpu.VMEM((rows, heads * dk), BF16),
            pltpu.VMEM((rows, heads * dv), BF16),
            pltpu.VMEM((rows, heads * dk), BF16),
            pltpu.VMEM((rows, heads * dv), F32),
            pltpu.VMEM((PIECES, dk, pw), F32),
            pltpu.VMEM((rows, dk), BF16),
            pltpu.VMEM((rows, rows), BF16),
            passed,
            passed,
            passed,
            passed,
            pltpu.VMEM((rows, heads), F32),
            pltpu.VMEM((rows, heads), F32),
            pltpu.VMEM((heads, rows), F32),
            pltpu.VMEM((heads, rows), F32),
            pltpu.VMEM((heads, rows, BLK), F32),
            pltpu.VMEM((heads, rows, BLK), F32),
            pltpu.VMEM((2, rows, BLK), F32),
            header,
            header,
            header,
            header,
            header,
            pltpu.VMEM((6, heads, dk), F32),
            sems,
            sems,
            sems,
            sems,
            sems,
            pltpu.SemaphoreType.DMA((5,)),
        ],
        compiler_params=pltpu.CompilerParams(
            collective_id=0, has_side_effects=True, vmem_limit_bytes=60 * 1024 * 1024
        ),
    )(*args[:3], args[3].transpose(1, 0, 2), *args[4:7], args[7].T, args[8].T)


def solution(mesh):
    rows = ("grp", "ctx", "head")
    placed = tuple(P(rows, *([None] * (n - 1))) for n in (2, 2, 2, 3, 2, 2, 2, 2, 2))
    return jax.shard_map(
        functools.partial(body, mesh.shape["ctx"], mesh.shape["head"]),
        mesh=mesh, in_specs=placed, out_specs=P(rows, None), check_vma=False,
    )
```

```python
import functools
import math

import jax
import jax.numpy as jnp
from jax import lax
from jax.experimental import pallas as pl
from jax.experimental.pallas import tpu as pltpu
from jax.sharding import PartitionSpec as P

BLK = 128
PIECES = 4
NEG_FILL = -1e30
MESH = pl.DeviceIdType.MESH
F32 = jnp.float32
BF16 = jnp.bfloat16


def kernel(
    sizes,
    q_any,
    k_any,
    v_any,
    scale_ref,
    ft_ref,
    fo_ref,
    fb_ref,
    ig_ref,
    fg_ref,
    out_any,
    out_ref,
    out_s,
    q_ref,
    k_ref,
    v_ref,
    in_s,
    qd,
    kd,
    vd,
    wk,
    num,
    state,
    lifted,
    inner,
    up_buf,
    tot_buf,
    bcol,
    wcol,
    brow,
    grow,
    peak_l,
    den_l,
    fin,
    own_h,
    up_h,
    tot_h,
    wts,
    up_s,
    up_r,
    hs,
):
    heads, dk, dv, nc, nz = sizes
    rows = q_ref.shape[0]
    k_in = pltpu.make_async_copy(k_any, k_ref, in_s.at[0])
    v_in = pltpu.make_async_copy(v_any, v_ref, in_s.at[1])
    q_in = pltpu.make_async_copy(q_any, q_ref, in_s.at[2])
    k_in.start()
    v_in.start()
    q_in.start()
    pw = dv // PIECES
    pieces = heads * PIECES
    factor = 1.0 / math.sqrt(dk)
    g, c, z = lax.axis_index("grp"), lax.axis_index("ctx"), lax.axis_index("head")
    place = c * nz + z
    has_up, has_down = place < nc * nz - 1, place > 0
    onward, prior = jnp.minimum(place + 1, nc * nz - 1), jnp.maximum(place - 1, 0)
    above = (g, lax.div(onward, nz), lax.rem(onward, nz))
    below = (g, lax.div(prior, nz), lax.rem(prior, nz))

    barrier = pltpu.get_barrier_semaphore()
    greet = ((has_up, above), (has_down, below))
    for there, who in greet:

        @pl.when(there)
        def _(who=who):
            pl.semaphore_signal(barrier, inc=1, device_id=who, device_id_type=MESH)

    def remote(src, dst, ssem, rsem, who):
        return pltpu.make_async_remote_copy(
            src_ref=src, dst_ref=dst, send_sem=ssem, recv_sem=rsem,
            device_id=who, device_id_type=MESH,
        )

    def up_copy(i):
        return remote(tot_buf.at[i], up_buf.at[i], up_s.at[i], up_r.at[i], above)

    up_head = remote(tot_h, up_h, hs.at[0], hs.at[1], above)

    token = lax.broadcasted_iota(jnp.int32, (BLK, 1), 0)

    def dequant(codes, e, h, width, kept):
        col = lax.broadcasted_iota(jnp.int32, (BLK, width), 1)
        start = pl.multiple_of(h * width, width)
        for b in range(rows // BLK):
            place = (pl.ds(b * BLK, BLK), pl.ds(start, width))
            off = fo_ref[b, h]
            bit = fb_ref[b, h]
            flip = jnp.where(bit >= 1, -2.0, -1.0)
            flip = flip * jnp.where(bit >= 2, 2.0, 1.0) * jnp.where(bit >= 3, 2.0, 1.0)
            flip = jnp.where(ft_ref[b, h] == e, flip, 1.0)
            hit = lax.rem(lax.rem(off, dv), width)
            line = jnp.where(token == lax.div(off, dv), hit, -1)
            scale = scale_ref[e, b, h]
            times = jnp.where(col == line, scale * flip, scale)
            kept[place] = (codes[place].astype(F32) * times).astype(BF16)
        return start

    lane = lax.broadcasted_iota(jnp.int32, (rows, heads), 1)

    def column(ref, h):
        return jnp.sum(jnp.where(lane == h, ref[...], 0.0), axis=1, keepdims=True)

    line_t = lax.broadcasted_iota(jnp.int32, (rows, rows), 0)
    line_s = lax.broadcasted_iota(jnp.int32, (rows, rows), 1)
    forget = fg_ref[...].astype(F32)
    logf = -(jnp.maximum(-forget, 0.0) + jnp.log1p(jnp.exp(-jnp.abs(forget))))
    gate = ig_ref[...].astype(F32)
    running = jnp.dot(
        logf, (line_t <= line_s).astype(F32),
        preferred_element_type=F32, precision=lax.Precision.HIGHEST,
    )
    brow[...] = running
    bcol[...] = running.T
    grow[...] = gate
    total = running[:, rows - 1 : rows]
    exponent = total - running + gate
    peak = jnp.max(exponent, axis=1, keepdims=True)
    wcol[...] = jnp.exp(exponent - peak).T
    own_h[:, dk : 2 * dk] = jnp.broadcast_to(peak, (heads, dk))
    own_h[:, 2 * dk :] = jnp.broadcast_to(total, (heads, dk))

    k_in.wait()

    def keys(h, carry):
        start = dequant(k_ref, 1, h, dk, kd)
        place = (slice(None), pl.ds(start, dk))
        weighted = (kd[place].astype(F32) * column(wcol, h)).astype(BF16)
        wk[place] = weighted
        own_h[pl.ds(h, 1), pl.ds(0, dk)] = jnp.sum(weighted.astype(F32), axis=0, keepdims=True)
        return carry

    lax.fori_loop(0, heads, keys, 0, unroll=2)

    def empty_header(ref):
        ref[:, 0:dk] = jnp.zeros((heads, dk), F32)
        ref[:, dk : 2 * dk] = jnp.full((heads, dk), NEG_FILL, F32)
        ref[:, 2 * dk :] = jnp.zeros((heads, dk), F32)

    @pl.when(place == 0)
    def _():
        empty_header(up_h)
        up_buf[...] = jnp.zeros_like(up_buf)

    def join(first, later, dst, at):
        m1, m2, f2 = first[:, dk : 2 * dk], later[:, dk : 2 * dk], later[:, 2 * dk :]
        m = jnp.maximum(m1 + f2, m2)
        w1, w2 = jnp.exp(m1 + f2 - m), jnp.exp(m2 - m)
        wts[at] = w1
        wts[at + 1] = w2
        dst[:, 0:dk] = w1 * first[:, 0:dk] + w2 * later[:, 0:dk]
        dst[:, dk : 2 * dk] = m
        dst[:, 2 * dk :] = first[:, 2 * dk :] + f2

    def weight(at, h):
        return wts[at, pl.ds(h, 1), :][:, 0:pw]

    def local(h):
        start = dequant(q_ref, 0, h, dk, qd)
        place = (slice(None), pl.ds(start, dk))
        scores = lax.dot_general(
            qd[place], kd[place], (((1,), (1,)), ((), ())), preferred_element_type=F32
        ) * factor
        gaps = column(bcol, h) - brow[pl.ds(h, 1), :] + grow[pl.ds(h, 1), :]
        gaps = jnp.where(line_t >= line_s, gaps, NEG_FILL)
        top = jnp.max(gaps, axis=1, keepdims=True)
        product = jnp.exp(gaps - top) * scores
        peak_l[h] = jnp.broadcast_to(top, (rows, BLK))
        den_l[h] = jnp.broadcast_to(jnp.sum(product, axis=1, keepdims=True), (rows, BLK))
        inner[...] = product.astype(BF16)

    def local_values(h):
        wide = (slice(None), pl.ds(pl.multiple_of(h * dv, dv), dv))
        num[wide] = jnp.dot(inner[...], vd[wide], preferred_element_type=F32)

    def head_state(h):
        wide = (slice(None), pl.ds(pl.multiple_of(h * dv, dv), dv))
        found = lax.dot_general(
            wk[:, pl.ds(pl.multiple_of(h * dk, dk), dk)], vd[wide],
            (((0,), (0,)), ((), ())), preferred_element_type=F32,
        )
        for p in range(PIECES):
            state[h * PIECES + p] = found[:, p * pw : (p + 1) * pw]

    def upward(i):
        h = lax.div(i, PIECES)

        @pl.when(has_down)
        def _():
            up_copy(i).wait_recv()

        mine = state[i]
        tot_buf[i] = (weight(0, h) * up_buf[i].astype(F32) + weight(1, h) * mine).astype(BF16)

        @pl.when(has_up)
        def _():
            up_copy(i).start()

    def ready(h, carry):
        dequant(v_ref, 2, h, dv, vd)
        head_state(h)
        local(h)
        local_values(h)
        return carry

    def ahead(i, done):
        h, p = lax.div(i, PIECES) + done, lax.rem(i, PIECES)

        @pl.when((p == 0) & (h < heads))
        def _():
            dequant(v_ref, 2, h, dv, vd)

        @pl.when((p == min(1, PIECES - 1)) & (h < heads))
        def _():
            head_state(h)

        @pl.when((p == max(0, PIECES - 2)) & (h < heads))
        def _():
            local(h)

        @pl.when((p == PIECES - 1) & (h < heads))
        def _():
            local_values(h)

    def finish(j):
        h = lax.div(j, PIECES)

        @pl.when(lax.rem(j, PIECES) == 0)
        def _():
            place = (slice(None), pl.ds(pl.multiple_of(h * dk, dk), dk))
            header = up_h[pl.ds(h, 1), :]
            norm, m = header[:, 0:dk], header[:, dk : dk + BLK]
            inter = column(bcol, h) + m
            top = jnp.maximum(peak_l[h], inter)
            shrink = jnp.exp(peak_l[h] - top)
            lift = jnp.exp(inter - top) * factor
            raised = (qd[place].astype(F32) * lift[:, 0:1]).astype(BF16)
            lifted[...] = raised
            den = shrink * den_l[h] + jnp.sum(raised.astype(F32) * norm, axis=1, keepdims=True)
            fin[0] = shrink
            fin[1] = 1.0 / jnp.maximum(jnp.abs(den), 1.0)

        piece = pl.ds(pl.multiple_of(j * pw, pw), pw)
        above_line = num[:, piece] * fin[0][:, 0:1] + jnp.dot(
            lifted[...], up_buf[j], preferred_element_type=F32
        )
        out_ref[:, piece] = (above_line * fin[1][:, 0:1]).astype(BF16)

        @pl.when(lax.rem(j, PIECES) == PIECES - 1)
        def _():
            out_copy(h).start()

    def out_copy(h):
        wide = (slice(None), pl.ds(pl.multiple_of(h * dv, dv), dv))
        return pltpu.make_async_copy(out_ref.at[wide], out_any.at[wide], out_s.at[h])

    v_in.wait()
    q_in.wait()
    done = jnp.minimum(heads, 1 + lax.div(3 * place, 4))
    lax.fori_loop(0, done, ready, 0)

    greeted = sum(there.astype(jnp.int32) for there, _ in greet)
    pl.semaphore_wait(barrier, greeted)

    @pl.when(has_down)
    def _():
        up_head.wait_recv()

    join(up_h, own_h, tot_h, 0)

    @pl.when(has_up)
    def _():
        up_head.start()

    def step(t, carry):
        upward(t)
        ahead(t, done)
        finish(t)
        return carry

    lax.fori_loop(0, pieces, step, 0)

    @pl.when(has_up)
    def _():
        up_head.wait_send()

    def drain_out(h, carry):
        out_copy(h).wait()
        return carry

    lax.fori_loop(0, heads, drain_out, 0)

    def drain(i, carry):
        @pl.when(has_up)
        def _():
            up_copy(i).wait_send()

        return carry

    lax.fori_loop(0, pieces, drain, 0)


def body(nc, nz, *args):
    rows = args[0].shape[0]
    heads = args[3].shape[2]
    dk, dv = args[0].shape[1] // heads, args[2].shape[1] // heads
    pieces, pw = heads * PIECES, dv // PIECES
    vmem, smem = pl.BlockSpec(memory_space=pltpu.VMEM), pl.BlockSpec(memory_space=pltpu.SMEM)
    passed = pltpu.VMEM((pieces, dk, pw), BF16)
    header = pltpu.VMEM((heads, 3 * dk), F32)
    sems = pltpu.SemaphoreType.DMA((pieces,))
    return pl.pallas_call(
        functools.partial(kernel, (heads, dk, dv, nc, nz)),
        out_shape=jax.ShapeDtypeStruct((rows, heads * dv), BF16),
        in_specs=[pl.BlockSpec(memory_space=pl.ANY)] * 3 + [smem] * 4 + [vmem] * 2,
        out_specs=pl.BlockSpec(memory_space=pl.ANY),
        scratch_shapes=[
            pltpu.VMEM((rows, heads * dv), BF16),
            pltpu.SemaphoreType.DMA((heads,)),
            pltpu.VMEM((rows, heads * dk), BF16),
            pltpu.VMEM((rows, heads * dk), BF16),
            pltpu.VMEM((rows, heads * dv), BF16),
            pltpu.SemaphoreType.DMA((3,)),
            pltpu.VMEM((rows, heads * dk), BF16),
            pltpu.VMEM((rows, heads * dk), BF16),
            pltpu.VMEM((rows, heads * dv), BF16),
            pltpu.VMEM((rows, heads * dk), BF16),
            pltpu.VMEM((rows, heads * dv), F32),
            pltpu.VMEM((pieces, dk, pw), F32),
            pltpu.VMEM((rows, dk), BF16),
            pltpu.VMEM((rows, rows), BF16),
            passed,
            passed,
            pltpu.VMEM((rows, heads), F32),
            pltpu.VMEM((rows, heads), F32),
            pltpu.VMEM((heads, rows), F32),
            pltpu.VMEM((heads, rows), F32),
            pltpu.VMEM((heads, rows, BLK), F32),
            pltpu.VMEM((heads, rows, BLK), F32),
            pltpu.VMEM((2, rows, BLK), F32),
            header,
            header,
            header,
            pltpu.VMEM((2, heads, dk), F32),
            sems,
            sems,
            pltpu.SemaphoreType.DMA((2,)),
        ],
        compiler_params=pltpu.CompilerParams(
            collective_id=0, has_side_effects=True, vmem_limit_bytes=60 * 1024 * 1024
        ),
    )(*args[:3], args[3].transpose(1, 0, 2), *args[4:7], args[7].T, args[8].T)


def solution(mesh):
    rows = ("grp", "ctx", "head")
    placed = tuple(P(rows, *([None] * (n - 1))) for n in (2, 2, 2, 3, 2, 2, 2, 2, 2))
    return jax.shard_map(
        functools.partial(body, mesh.shape["ctx"], mesh.shape["head"]),
        mesh=mesh, in_specs=placed, out_specs=P(rows, None), check_vma=False,
    )
```

```python
import functools
import math

import jax
import jax.numpy as jnp
from jax import lax
from jax.experimental import pallas as pl
from jax.experimental.pallas import tpu as pltpu
from jax.sharding import PartitionSpec as P

BLK = 128
PIECES = 4
NEG_FILL = -1e30
MESH = pl.DeviceIdType.MESH
F32 = jnp.float32
BF16 = jnp.bfloat16


def kernel(
    sizes,
    q_any,
    k_any,
    v_any,
    scale_ref,
    ft_ref,
    fo_ref,
    fb_ref,
    ig_ref,
    fg_ref,
    out_any,
    out_ref,
    out_s,
    q_ref,
    k_ref,
    v_ref,
    in_s,
    qd,
    kd,
    vd,
    wk,
    num,
    state,
    lifted,
    inner,
    up_buf,
    tot_buf,
    bcol,
    wcol,
    brow,
    grow,
    peak_l,
    den_l,
    fin,
    own_h,
    up_h,
    tot_h,
    wts,
    up_s,
    up_r,
    hs,
):
    heads, dk, dv, nc, nz = sizes
    rows = q_ref.shape[0]
    k_in = pltpu.make_async_copy(k_any, k_ref, in_s.at[0])
    v_in = pltpu.make_async_copy(v_any, v_ref, in_s.at[1])
    q_in = pltpu.make_async_copy(q_any, q_ref, in_s.at[2])
    k_in.start()
    v_in.start()
    q_in.start()
    pw = dv // PIECES
    pieces = heads * PIECES
    factor = 1.0 / math.sqrt(dk)
    g, c, z = lax.axis_index("grp"), lax.axis_index("ctx"), lax.axis_index("head")
    place = c * nz + z
    has_up, has_down = place < nc * nz - 1, place > 0
    onward, prior = jnp.minimum(place + 1, nc * nz - 1), jnp.maximum(place - 1, 0)
    above = (g, lax.div(onward, nz), lax.rem(onward, nz))
    below = (g, lax.div(prior, nz), lax.rem(prior, nz))

    barrier = pltpu.get_barrier_semaphore()
    greet = ((has_up, above), (has_down, below))
    for there, who in greet:

        @pl.when(there)
        def _(who=who):
            pl.semaphore_signal(barrier, inc=1, device_id=who, device_id_type=MESH)

    def remote(src, dst, ssem, rsem, who):
        return pltpu.make_async_remote_copy(
            src_ref=src, dst_ref=dst, send_sem=ssem, recv_sem=rsem,
            device_id=who, device_id_type=MESH,
        )

    def up_copy(i):
        return remote(tot_buf.at[i], up_buf.at[i], up_s.at[i], up_r.at[i], above)

    up_head = remote(tot_h, up_h, hs.at[0], hs.at[1], above)

    token = lax.broadcasted_iota(jnp.int32, (BLK, 1), 0)

    def dequant(codes, e, h, width, kept):
        col = lax.broadcasted_iota(jnp.int32, (BLK, width), 1)
        start = pl.multiple_of(h * width, width)
        for b in range(rows // BLK):
            place = (pl.ds(b * BLK, BLK), pl.ds(start, width))
            off = fo_ref[b, h]
            bit = fb_ref[b, h]
            flip = jnp.where(bit >= 1, -2.0, -1.0)
            flip = flip * jnp.where(bit >= 2, 2.0, 1.0) * jnp.where(bit >= 3, 2.0, 1.0)
            flip = jnp.where(ft_ref[b, h] == e, flip, 1.0)
            hit = lax.rem(lax.rem(off, dv), width)
            line = jnp.where(token == lax.div(off, dv), hit, -1)
            scale = scale_ref[e, b, h]
            times = jnp.where(col == line, scale * flip, scale)
            kept[place] = (codes[place].astype(F32) * times).astype(BF16)
        return start

    lane = lax.broadcasted_iota(jnp.int32, (rows, heads), 1)

    def column(ref, h):
        return jnp.sum(jnp.where(lane == h, ref[...], 0.0), axis=1, keepdims=True)

    line_t = lax.broadcasted_iota(jnp.int32, (rows, rows), 0)
    line_s = lax.broadcasted_iota(jnp.int32, (rows, rows), 1)
    forget = fg_ref[...].astype(F32)
    logf = -(jnp.maximum(-forget, 0.0) + jnp.log1p(jnp.exp(-jnp.abs(forget))))
    gate = ig_ref[...].astype(F32)
    running = jnp.dot(
        logf, (line_t <= line_s).astype(F32),
        preferred_element_type=F32, precision=lax.Precision.HIGHEST,
    )
    brow[...] = running
    bcol[...] = running.T
    grow[...] = gate
    total = running[:, rows - 1 : rows]
    exponent = total - running + gate
    peak = jnp.max(exponent, axis=1, keepdims=True)
    wcol[...] = jnp.exp(exponent - peak).T
    own_h[:, dk : 2 * dk] = jnp.broadcast_to(peak, (heads, dk))
    own_h[:, 2 * dk :] = jnp.broadcast_to(total, (heads, dk))

    k_in.wait()

    def keys(h, carry):
        start = dequant(k_ref, 1, h, dk, kd)
        place = (slice(None), pl.ds(start, dk))
        weighted = (kd[place].astype(F32) * column(wcol, h)).astype(BF16)
        wk[place] = weighted
        own_h[pl.ds(h, 1), pl.ds(0, dk)] = jnp.sum(weighted.astype(F32), axis=0, keepdims=True)
        return carry

    lax.fori_loop(0, heads, keys, 0, unroll=2)

    def empty_header(ref):
        ref[:, 0:dk] = jnp.zeros((heads, dk), F32)
        ref[:, dk : 2 * dk] = jnp.full((heads, dk), NEG_FILL, F32)
        ref[:, 2 * dk :] = jnp.zeros((heads, dk), F32)

    @pl.when(place == 0)
    def _():
        empty_header(up_h)
        up_buf[...] = jnp.zeros_like(up_buf)

    def join(first, later, dst, at):
        m1, m2, f2 = first[:, dk : 2 * dk], later[:, dk : 2 * dk], later[:, 2 * dk :]
        m = jnp.maximum(m1 + f2, m2)
        w1, w2 = jnp.exp(m1 + f2 - m), jnp.exp(m2 - m)
        wts[at] = w1
        wts[at + 1] = w2
        dst[:, 0:dk] = w1 * first[:, 0:dk] + w2 * later[:, 0:dk]
        dst[:, dk : 2 * dk] = m
        dst[:, 2 * dk :] = first[:, 2 * dk :] + f2

    def weight(at, h):
        return wts[at, pl.ds(h, 1), :][:, 0:pw]

    def local(h):
        start = dequant(q_ref, 0, h, dk, qd)
        place = (slice(None), pl.ds(start, dk))
        scores = lax.dot_general(
            qd[place], kd[place], (((1,), (1,)), ((), ())), preferred_element_type=F32
        ) * factor
        gaps = column(bcol, h) - brow[pl.ds(h, 1), :] + grow[pl.ds(h, 1), :]
        gaps = jnp.where(line_t >= line_s, gaps, NEG_FILL)
        top = jnp.max(gaps, axis=1, keepdims=True)
        product = jnp.exp(gaps - top) * scores
        peak_l[h] = jnp.broadcast_to(top, (rows, BLK))
        den_l[h] = jnp.broadcast_to(jnp.sum(product, axis=1, keepdims=True), (rows, BLK))
        inner[...] = product.astype(BF16)

    def local_values(h):
        wide = (slice(None), pl.ds(pl.multiple_of(h * dv, dv), dv))
        num[wide] = jnp.dot(inner[...], vd[wide], preferred_element_type=F32)

    def head_state(h):
        wide = (slice(None), pl.ds(pl.multiple_of(h * dv, dv), dv))
        found = lax.dot_general(
            wk[:, pl.ds(pl.multiple_of(h * dk, dk), dk)], vd[wide],
            (((0,), (0,)), ((), ())), preferred_element_type=F32,
        )
        for p in range(PIECES):
            state[h * PIECES + p] = found[:, p * pw : (p + 1) * pw]

    def upward(i):
        h = lax.div(i, PIECES)

        @pl.when(has_down)
        def _():
            up_copy(i).wait_recv()

        mine = state[i]
        tot_buf[i] = (weight(0, h) * up_buf[i].astype(F32) + weight(1, h) * mine).astype(BF16)

        @pl.when(has_up)
        def _():
            up_copy(i).start()

    def states(h, carry):
        dequant(v_ref, 2, h, dv, vd)
        head_state(h)
        return carry

    def locals_of(h, carry):
        local(h)
        local_values(h)
        return carry

    def ahead(i, done):
        h, p = lax.div(i, PIECES) + done, lax.rem(i, PIECES)

        @pl.when((p == 0) & (h < heads))
        def _():
            dequant(v_ref, 2, h, dv, vd)

        @pl.when((p == min(1, PIECES - 1)) & (h < heads))
        def _():
            head_state(h)

    def finish(j):
        h = lax.div(j, PIECES)

        @pl.when(lax.rem(j, PIECES) == 0)
        def _():
            place = (slice(None), pl.ds(pl.multiple_of(h * dk, dk), dk))
            header = up_h[pl.ds(h, 1), :]
            norm, m = header[:, 0:dk], header[:, dk : dk + BLK]
            inter = column(bcol, h) + m
            top = jnp.maximum(peak_l[h], inter)
            shrink = jnp.exp(peak_l[h] - top)
            lift = jnp.exp(inter - top) * factor
            raised = (qd[place].astype(F32) * lift[:, 0:1]).astype(BF16)
            lifted[...] = raised
            den = shrink * den_l[h] + jnp.sum(raised.astype(F32) * norm, axis=1, keepdims=True)
            fin[0] = shrink
            fin[1] = 1.0 / jnp.maximum(jnp.abs(den), 1.0)

        piece = pl.ds(pl.multiple_of(j * pw, pw), pw)
        above_line = num[:, piece] * fin[0][:, 0:1] + jnp.dot(
            lifted[...], up_buf[j], preferred_element_type=F32
        )
        out_ref[:, piece] = (above_line * fin[1][:, 0:1]).astype(BF16)

        @pl.when(lax.rem(j, PIECES) == PIECES - 1)
        def _():
            out_copy(h).start()

    def out_copy(h):
        wide = (slice(None), pl.ds(pl.multiple_of(h * dv, dv), dv))
        return pltpu.make_async_copy(out_ref.at[wide], out_any.at[wide], out_s.at[h])

    v_in.wait()
    q_in.wait()
    early = 2 * place < nc * nz
    done = jnp.minimum(heads, 1 + jnp.where(early, place, heads))
    lax.fori_loop(0, done, states, 0)

    @pl.when(jnp.logical_not(early))
    def _():
        lax.fori_loop(0, heads, locals_of, 0)

    greeted = sum(there.astype(jnp.int32) for there, _ in greet)
    pl.semaphore_wait(barrier, greeted)

    @pl.when(has_down)
    def _():
        up_head.wait_recv()

    join(up_h, own_h, tot_h, 0)

    @pl.when(has_up)
    def _():
        up_head.start()

    def step(t, carry):
        upward(t)

        @pl.when(early)
        def _():
            ahead(t, done)

        @pl.when(jnp.logical_not(early))
        def _():
            finish(t)

        return carry

    lax.fori_loop(0, pieces, step, 0)

    @pl.when(early)
    def _():
        lax.fori_loop(0, heads, locals_of, 0)

        def rest(t, carry):
            finish(t)
            return carry

        lax.fori_loop(0, pieces, rest, 0)

    @pl.when(has_up)
    def _():
        up_head.wait_send()

    def drain_out(h, carry):
        out_copy(h).wait()
        return carry

    lax.fori_loop(0, heads, drain_out, 0)

    def drain(i, carry):
        @pl.when(has_up)
        def _():
            up_copy(i).wait_send()

        return carry

    lax.fori_loop(0, pieces, drain, 0)


def body(nc, nz, *args):
    rows = args[0].shape[0]
    heads = args[3].shape[2]
    dk, dv = args[0].shape[1] // heads, args[2].shape[1] // heads
    pieces, pw = heads * PIECES, dv // PIECES
    vmem, smem = pl.BlockSpec(memory_space=pltpu.VMEM), pl.BlockSpec(memory_space=pltpu.SMEM)
    passed = pltpu.VMEM((pieces, dk, pw), BF16)
    header = pltpu.VMEM((heads, 3 * dk), F32)
    sems = pltpu.SemaphoreType.DMA((pieces,))
    return pl.pallas_call(
        functools.partial(kernel, (heads, dk, dv, nc, nz)),
        out_shape=jax.ShapeDtypeStruct((rows, heads * dv), BF16),
        in_specs=[pl.BlockSpec(memory_space=pl.ANY)] * 3 + [smem] * 4 + [vmem] * 2,
        out_specs=pl.BlockSpec(memory_space=pl.ANY),
        scratch_shapes=[
            pltpu.VMEM((rows, heads * dv), BF16),
            pltpu.SemaphoreType.DMA((heads,)),
            pltpu.VMEM((rows, heads * dk), BF16),
            pltpu.VMEM((rows, heads * dk), BF16),
            pltpu.VMEM((rows, heads * dv), BF16),
            pltpu.SemaphoreType.DMA((3,)),
            pltpu.VMEM((rows, heads * dk), BF16),
            pltpu.VMEM((rows, heads * dk), BF16),
            pltpu.VMEM((rows, heads * dv), BF16),
            pltpu.VMEM((rows, heads * dk), BF16),
            pltpu.VMEM((rows, heads * dv), F32),
            pltpu.VMEM((pieces, dk, pw), F32),
            pltpu.VMEM((rows, dk), BF16),
            pltpu.VMEM((rows, rows), BF16),
            passed,
            passed,
            pltpu.VMEM((rows, heads), F32),
            pltpu.VMEM((rows, heads), F32),
            pltpu.VMEM((heads, rows), F32),
            pltpu.VMEM((heads, rows), F32),
            pltpu.VMEM((heads, rows, BLK), F32),
            pltpu.VMEM((heads, rows, BLK), F32),
            pltpu.VMEM((2, rows, BLK), F32),
            header,
            header,
            header,
            pltpu.VMEM((2, heads, dk), F32),
            sems,
            sems,
            pltpu.SemaphoreType.DMA((2,)),
        ],
        compiler_params=pltpu.CompilerParams(
            collective_id=0, has_side_effects=True, vmem_limit_bytes=60 * 1024 * 1024
        ),
    )(*args[:3], args[3].transpose(1, 0, 2), *args[4:7], args[7].T, args[8].T)


def solution(mesh):
    rows = ("grp", "ctx", "head")
    placed = tuple(P(rows, *([None] * (n - 1))) for n in (2, 2, 2, 3, 2, 2, 2, 2, 2))
    return jax.shard_map(
        functools.partial(body, mesh.shape["ctx"], mesh.shape["head"]),
        mesh=mesh, in_specs=placed, out_specs=P(rows, None), check_vma=False,
    )
```

```python
import functools
import math

import jax
import jax.numpy as jnp
from jax import lax
from jax.experimental import pallas as pl
from jax.experimental.pallas import tpu as pltpu
from jax.sharding import PartitionSpec as P

BLK = 128
PIECES = 4
NEG_FILL = -1e30
MESH = pl.DeviceIdType.MESH
F32 = jnp.float32
BF16 = jnp.bfloat16


def kernel(
    sizes,
    q_any,
    k_any,
    v_any,
    scale_ref,
    ft_ref,
    fo_ref,
    fb_ref,
    ig_ref,
    fg_ref,
    out_any,
    out_ref,
    out_s,
    q_ref,
    k_ref,
    v_ref,
    in_s,
    qd,
    kd,
    vd,
    wk,
    num,
    state,
    lifted,
    inner,
    up_buf,
    tot_buf,
    relay,
    bcol,
    wcol,
    brow,
    grow,
    peak_l,
    den_l,
    fin,
    own_h,
    up_h,
    tot_h,
    wts,
    up_s,
    up_r,
    rl_s,
    rl_r,
    hs,
):
    heads, dk, dv, nc, nz = sizes
    rows = q_ref.shape[0]
    k_in = pltpu.make_async_copy(k_any, k_ref, in_s.at[0])
    v_in = pltpu.make_async_copy(v_any, v_ref, in_s.at[1])
    q_in = pltpu.make_async_copy(q_any, q_ref, in_s.at[2])
    k_in.start()
    v_in.start()
    q_in.start()
    pw = dv // PIECES
    pieces = heads * PIECES
    factor = 1.0 / math.sqrt(dk)
    g, c, z = lax.axis_index("grp"), lax.axis_index("ctx"), lax.axis_index("head")
    place = c * nz + z
    has_up, has_down = place < nc * nz - 1, place > 0
    onward, prior = jnp.minimum(place + 1, nc * nz - 1), jnp.maximum(place - 1, 0)
    above = (g, lax.div(onward, nz), lax.rem(onward, nz))
    below = (g, lax.div(prior, nz), lax.rem(prior, nz))

    barrier = pltpu.get_barrier_semaphore()
    mid = nc * nz // 2 - 1
    first = (g, 0, 0)
    half = (g, mid // nz, mid % nz)
    over = (g, (mid + 1) // nz, (mid + 1) % nz)
    is_first, is_half, is_over = place == 0, place == mid, place == mid + 1
    direct = has_up & (place != mid)
    greet = (
        (has_up, above), (has_down, below), (is_half, first), (is_over, first),
        (is_first, half), (is_first, over),
    )
    for there, who in greet:

        @pl.when(there)
        def _(who=who):
            pl.semaphore_signal(barrier, inc=1, device_id=who, device_id_type=MESH)

    def remote(src, dst, ssem, rsem, who):
        return pltpu.make_async_remote_copy(
            src_ref=src, dst_ref=dst, send_sem=ssem, recv_sem=rsem,
            device_id=who, device_id_type=MESH,
        )

    def up_copy(i):
        return remote(tot_buf.at[i], up_buf.at[i], up_s.at[i], up_r.at[i], above)

    def relay_copy(i):
        return remote(tot_buf.at[i], relay.at[i], up_s.at[i], rl_r.at[i], first)

    def relay_on(i):
        return remote(relay.at[i], up_buf.at[i], rl_s.at[i], up_r.at[i], over)

    up_head = remote(tot_h, up_h, hs.at[0], hs.at[1], above)

    token = lax.broadcasted_iota(jnp.int32, (BLK, 1), 0)

    def dequant(codes, e, h, width, kept):
        col = lax.broadcasted_iota(jnp.int32, (BLK, width), 1)
        start = pl.multiple_of(h * width, width)
        for b in range(rows // BLK):
            place = (pl.ds(b * BLK, BLK), pl.ds(start, width))
            off = fo_ref[b, h]
            bit = fb_ref[b, h]
            flip = jnp.where(bit >= 1, -2.0, -1.0)
            flip = flip * jnp.where(bit >= 2, 2.0, 1.0) * jnp.where(bit >= 3, 2.0, 1.0)
            flip = jnp.where(ft_ref[b, h] == e, flip, 1.0)
            hit = lax.rem(lax.rem(off, dv), width)
            line = jnp.where(token == lax.div(off, dv), hit, -1)
            scale = scale_ref[e, b, h]
            times = jnp.where(col == line, scale * flip, scale)
            kept[place] = (codes[place].astype(F32) * times).astype(BF16)
        return start

    lane = lax.broadcasted_iota(jnp.int32, (rows, heads), 1)

    def column(ref, h):
        return jnp.sum(jnp.where(lane == h, ref[...], 0.0), axis=1, keepdims=True)

    line_t = lax.broadcasted_iota(jnp.int32, (rows, rows), 0)
    line_s = lax.broadcasted_iota(jnp.int32, (rows, rows), 1)
    forget = fg_ref[...].astype(F32)
    logf = -(jnp.maximum(-forget, 0.0) + jnp.log1p(jnp.exp(-jnp.abs(forget))))
    gate = ig_ref[...].astype(F32)
    running = jnp.dot(
        logf, (line_t <= line_s).astype(F32),
        preferred_element_type=F32, precision=lax.Precision.HIGHEST,
    )
    brow[...] = running
    bcol[...] = running.T
    grow[...] = gate
    total = running[:, rows - 1 : rows]
    exponent = total - running + gate
    peak = jnp.max(exponent, axis=1, keepdims=True)
    wcol[...] = jnp.exp(exponent - peak).T
    own_h[:, dk : 2 * dk] = jnp.broadcast_to(peak, (heads, dk))
    own_h[:, 2 * dk :] = jnp.broadcast_to(total, (heads, dk))

    k_in.wait()

    def keys(h, carry):
        start = dequant(k_ref, 1, h, dk, kd)
        place = (slice(None), pl.ds(start, dk))
        weighted = (kd[place].astype(F32) * column(wcol, h)).astype(BF16)
        wk[place] = weighted
        own_h[pl.ds(h, 1), pl.ds(0, dk)] = jnp.sum(weighted.astype(F32), axis=0, keepdims=True)
        return carry

    lax.fori_loop(0, heads, keys, 0, unroll=2)

    def empty_header(ref):
        ref[:, 0:dk] = jnp.zeros((heads, dk), F32)
        ref[:, dk : 2 * dk] = jnp.full((heads, dk), NEG_FILL, F32)
        ref[:, 2 * dk :] = jnp.zeros((heads, dk), F32)

    @pl.when(place == 0)
    def _():
        empty_header(up_h)
        up_buf[...] = jnp.zeros_like(up_buf)

    def join(first, later, dst, at):
        m1, m2, f2 = first[:, dk : 2 * dk], later[:, dk : 2 * dk], later[:, 2 * dk :]
        m = jnp.maximum(m1 + f2, m2)
        w1, w2 = jnp.exp(m1 + f2 - m), jnp.exp(m2 - m)
        wts[at] = w1
        wts[at + 1] = w2
        dst[:, 0:dk] = w1 * first[:, 0:dk] + w2 * later[:, 0:dk]
        dst[:, dk : 2 * dk] = m
        dst[:, 2 * dk :] = first[:, 2 * dk :] + f2

    def weight(at, h):
        return wts[at, pl.ds(h, 1), :][:, 0:pw]

    def local(h):
        start = dequant(q_ref, 0, h, dk, qd)
        place = (slice(None), pl.ds(start, dk))
        scores = lax.dot_general(
            qd[place], kd[place], (((1,), (1,)), ((), ())), preferred_element_type=F32
        ) * factor
        gaps = column(bcol, h) - brow[pl.ds(h, 1), :] + grow[pl.ds(h, 1), :]
        gaps = jnp.where(line_t >= line_s, gaps, NEG_FILL)
        top = jnp.max(gaps, axis=1, keepdims=True)
        product = jnp.exp(gaps - top) * scores
        peak_l[h] = jnp.broadcast_to(top, (rows, BLK))
        den_l[h] = jnp.broadcast_to(jnp.sum(product, axis=1, keepdims=True), (rows, BLK))
        inner[...] = product.astype(BF16)

    def local_values(h):
        wide = (slice(None), pl.ds(pl.multiple_of(h * dv, dv), dv))
        num[wide] = jnp.dot(inner[...], vd[wide], preferred_element_type=F32)

    def head_state(h):
        wide = (slice(None), pl.ds(pl.multiple_of(h * dv, dv), dv))
        found = lax.dot_general(
            wk[:, pl.ds(pl.multiple_of(h * dk, dk), dk)], vd[wide],
            (((0,), (0,)), ((), ())), preferred_element_type=F32,
        )
        for p in range(PIECES):
            state[h * PIECES + p] = found[:, p * pw : (p + 1) * pw]

    def upward(i):
        h = lax.div(i, PIECES)

        @pl.when(has_down)
        def _():
            up_copy(i).wait_recv()

        mine = state[i]
        tot_buf[i] = (weight(0, h) * up_buf[i].astype(F32) + weight(1, h) * mine).astype(BF16)

        @pl.when(direct)
        def _():
            up_copy(i).start()

        @pl.when(is_half)
        def _():
            relay_copy(i).start()

    def states(h, carry):
        dequant(v_ref, 2, h, dv, vd)
        head_state(h)
        return carry

    def locals_of(h, carry):
        local(h)
        local_values(h)
        return carry

    def ahead(i, done):
        h, p = lax.div(i, PIECES) + done, lax.rem(i, PIECES)

        @pl.when((p == 0) & (h < heads))
        def _():
            dequant(v_ref, 2, h, dv, vd)

        @pl.when((p == min(1, PIECES - 1)) & (h < heads))
        def _():
            head_state(h)

    def finish(j):
        h = lax.div(j, PIECES)

        @pl.when(lax.rem(j, PIECES) == 0)
        def _():
            place = (slice(None), pl.ds(pl.multiple_of(h * dk, dk), dk))
            header = up_h[pl.ds(h, 1), :]
            norm, m = header[:, 0:dk], header[:, dk : dk + BLK]
            inter = column(bcol, h) + m
            top = jnp.maximum(peak_l[h], inter)
            shrink = jnp.exp(peak_l[h] - top)
            lift = jnp.exp(inter - top) * factor
            raised = (qd[place].astype(F32) * lift[:, 0:1]).astype(BF16)
            lifted[...] = raised
            den = shrink * den_l[h] + jnp.sum(raised.astype(F32) * norm, axis=1, keepdims=True)
            fin[0] = shrink
            fin[1] = 1.0 / jnp.maximum(jnp.abs(den), 1.0)

        piece = pl.ds(pl.multiple_of(j * pw, pw), pw)
        above_line = num[:, piece] * fin[0][:, 0:1] + jnp.dot(
            lifted[...], up_buf[j], preferred_element_type=F32
        )
        out_ref[:, piece] = (above_line * fin[1][:, 0:1]).astype(BF16)

        @pl.when(lax.rem(j, PIECES) == PIECES - 1)
        def _():
            out_copy(h).start()

    def out_copy(h):
        wide = (slice(None), pl.ds(pl.multiple_of(h * dv, dv), dv))
        return pltpu.make_async_copy(out_ref.at[wide], out_any.at[wide], out_s.at[h])

    v_in.wait()
    q_in.wait()
    early = 2 * place < nc * nz
    done = jnp.minimum(heads, 1 + jnp.where(early, place, heads))
    lax.fori_loop(0, done, states, 0)

    @pl.when(jnp.logical_not(early))
    def _():
        lax.fori_loop(0, heads, locals_of, 0)

    greeted = sum(there.astype(jnp.int32) for there, _ in greet)
    pl.semaphore_wait(barrier, greeted)

    @pl.when(has_down)
    def _():
        up_head.wait_recv()

    join(up_h, own_h, tot_h, 0)

    @pl.when(has_up)
    def _():
        up_head.start()

    def step(t, carry):
        upward(t)

        @pl.when(early)
        def _():
            ahead(t, done)

        @pl.when(jnp.logical_not(early))
        def _():
            finish(t)

        return carry

    lax.fori_loop(0, pieces, step, 0)

    @pl.when(is_first)
    def _():
        def pass_on(i, carry):
            relay_copy(i).wait_recv()
            relay_on(i).start()
            return carry

        lax.fori_loop(0, pieces, pass_on, 0)

    @pl.when(early)
    def _():
        lax.fori_loop(0, heads, locals_of, 0)

        def rest(t, carry):
            finish(t)
            return carry

        lax.fori_loop(0, pieces, rest, 0)

    @pl.when(has_up)
    def _():
        up_head.wait_send()

    def drain_out(h, carry):
        out_copy(h).wait()
        return carry

    lax.fori_loop(0, heads, drain_out, 0)

    def drain(i, carry):
        @pl.when(direct)
        def _():
            up_copy(i).wait_send()

        @pl.when(is_half)
        def _():
            relay_copy(i).wait_send()

        @pl.when(is_first)
        def _():
            relay_on(i).wait_send()

        return carry

    lax.fori_loop(0, pieces, drain, 0)


def body(nc, nz, *args):
    rows = args[0].shape[0]
    heads = args[3].shape[2]
    dk, dv = args[0].shape[1] // heads, args[2].shape[1] // heads
    pieces, pw = heads * PIECES, dv // PIECES
    vmem, smem = pl.BlockSpec(memory_space=pltpu.VMEM), pl.BlockSpec(memory_space=pltpu.SMEM)
    passed = pltpu.VMEM((pieces, dk, pw), BF16)
    header = pltpu.VMEM((heads, 3 * dk), F32)
    sems = pltpu.SemaphoreType.DMA((pieces,))
    return pl.pallas_call(
        functools.partial(kernel, (heads, dk, dv, nc, nz)),
        out_shape=jax.ShapeDtypeStruct((rows, heads * dv), BF16),
        in_specs=[pl.BlockSpec(memory_space=pl.ANY)] * 3 + [smem] * 4 + [vmem] * 2,
        out_specs=pl.BlockSpec(memory_space=pl.ANY),
        scratch_shapes=[
            pltpu.VMEM((rows, heads * dv), BF16),
            pltpu.SemaphoreType.DMA((heads,)),
            pltpu.VMEM((rows, heads * dk), BF16),
            pltpu.VMEM((rows, heads * dk), BF16),
            pltpu.VMEM((rows, heads * dv), BF16),
            pltpu.SemaphoreType.DMA((3,)),
            pltpu.VMEM((rows, heads * dk), BF16),
            pltpu.VMEM((rows, heads * dk), BF16),
            pltpu.VMEM((rows, heads * dv), BF16),
            pltpu.VMEM((rows, heads * dk), BF16),
            pltpu.VMEM((rows, heads * dv), F32),
            pltpu.VMEM((pieces, dk, pw), F32),
            pltpu.VMEM((rows, dk), BF16),
            pltpu.VMEM((rows, rows), BF16),
            passed,
            passed,
            passed,
            pltpu.VMEM((rows, heads), F32),
            pltpu.VMEM((rows, heads), F32),
            pltpu.VMEM((heads, rows), F32),
            pltpu.VMEM((heads, rows), F32),
            pltpu.VMEM((heads, rows, BLK), F32),
            pltpu.VMEM((heads, rows, BLK), F32),
            pltpu.VMEM((2, rows, BLK), F32),
            header,
            header,
            header,
            pltpu.VMEM((2, heads, dk), F32),
            sems,
            sems,
            sems,
            sems,
            pltpu.SemaphoreType.DMA((2,)),
        ],
        compiler_params=pltpu.CompilerParams(
            collective_id=0, has_side_effects=True, vmem_limit_bytes=60 * 1024 * 1024
        ),
    )(*args[:3], args[3].transpose(1, 0, 2), *args[4:7], args[7].T, args[8].T)


def solution(mesh):
    rows = ("grp", "ctx", "head")
    placed = tuple(P(rows, *([None] * (n - 1))) for n in (2, 2, 2, 3, 2, 2, 2, 2, 2))
    return jax.shard_map(
        functools.partial(body, mesh.shape["ctx"], mesh.shape["head"]),
        mesh=mesh, in_specs=placed, out_specs=P(rows, None), check_vma=False,
    )
```

```python
import functools
import math

import jax
import jax.numpy as jnp
from jax import lax
from jax.experimental import pallas as pl
from jax.experimental.pallas import tpu as pltpu
from jax.sharding import PartitionSpec as P

BLK = 128
PIECES = 4
Z_SKEW = 5
C_SKEW = 3
NEG_FILL = -1e30
MESH = pl.DeviceIdType.MESH
F32 = jnp.float32
BF16 = jnp.bfloat16


def kernel(
    sizes,
    q_any,
    k_any,
    v_any,
    scale_ref,
    ft_ref,
    fo_ref,
    fb_ref,
    ig_ref,
    fg_ref,
    out_any,
    out_ref,
    out_s,
    q_ref,
    k_ref,
    v_ref,
    in_s,
    qd,
    kd,
    vd,
    wk,
    num,
    state,
    lifted,
    inner,
    up_buf,
    tot_buf,
    r_buf,
    rs_buf,
    bcol,
    wcol,
    brow,
    grow,
    peak_l,
    den_l,
    fin,
    own_h,
    up_h,
    tot_h,
    r_h,
    rs_h,
    wts,
    up_s,
    up_r,
    dn_s,
    r_r,
    cx_s,
    hs,
):
    heads, dk, dv, nc, nz = sizes
    rows = q_ref.shape[0]
    k_in = pltpu.make_async_copy(k_any, k_ref, in_s.at[0])
    v_in = pltpu.make_async_copy(v_any, v_ref, in_s.at[1])
    q_in = pltpu.make_async_copy(q_any, q_ref, in_s.at[2])
    k_in.start()
    v_in.start()
    q_in.start()
    pw = dv // PIECES
    pieces = heads * PIECES
    factor = 1.0 / math.sqrt(dk)
    g, c, z = lax.axis_index("grp"), lax.axis_index("ctx"), lax.axis_index("head")
    last = nz - 1
    has_up, has_down = z < last, z > 0
    at_end = z == last
    gives_row, has_row = at_end & (c < nc - 1), c > 0
    above = (g, c, jnp.minimum(z + 1, last))
    below = (g, c, jnp.maximum(z - 1, 0))
    after = (g, jnp.minimum(c + 1, nc - 1), z)
    earlier = (g, jnp.maximum(c - 1, 0), z)

    barrier = pltpu.get_barrier_semaphore()
    greet = ((has_up, above), (has_down, below), (gives_row, after), (at_end & has_row, earlier))
    for there, who in greet:

        @pl.when(there)
        def _(who=who):
            pl.semaphore_signal(barrier, inc=1, device_id=who, device_id_type=MESH)

    def remote(src, dst, ssem, rsem, who):
        return pltpu.make_async_remote_copy(
            src_ref=src, dst_ref=dst, send_sem=ssem, recv_sem=rsem,
            device_id=who, device_id_type=MESH,
        )

    def up_copy(i):
        return remote(tot_buf.at[i], up_buf.at[i], up_s.at[i], up_r.at[i], above)

    def down_copy(i):
        return remote(r_buf.at[i], r_buf.at[i], dn_s.at[i], r_r.at[i], below)

    def row_copy(i):
        return remote(rs_buf.at[i], r_buf.at[i], cx_s.at[i], r_r.at[i], after)

    up_head = remote(tot_h, up_h, hs.at[0], hs.at[1], above)
    down_head = remote(r_h, r_h, hs.at[2], hs.at[3], below)
    row_head = remote(rs_h, r_h, hs.at[4], hs.at[3], after)

    token = lax.broadcasted_iota(jnp.int32, (BLK, 1), 0)

    def dequant(codes, e, h, width, kept):
        col = lax.broadcasted_iota(jnp.int32, (BLK, width), 1)
        start = pl.multiple_of(h * width, width)
        for b in range(rows // BLK):
            place = (pl.ds(b * BLK, BLK), pl.ds(start, width))
            off = fo_ref[b, h]
            bit = fb_ref[b, h]
            flip = jnp.where(bit >= 1, -2.0, -1.0)
            flip = flip * jnp.where(bit >= 2, 2.0, 1.0) * jnp.where(bit >= 3, 2.0, 1.0)
            flip = jnp.where(ft_ref[b, h] == e, flip, 1.0)
            hit = lax.rem(lax.rem(off, dv), width)
            line = jnp.where(token == lax.div(off, dv), hit, -1)
            scale = scale_ref[e, b, h]
            times = jnp.where(col == line, scale * flip, scale)
            kept[place] = (codes[place].astype(F32) * times).astype(BF16)
        return start

    lane = lax.broadcasted_iota(jnp.int32, (rows, heads), 1)

    def column(ref, h):
        return jnp.sum(jnp.where(lane == h, ref[...], 0.0), axis=1, keepdims=True)

    line_t = lax.broadcasted_iota(jnp.int32, (rows, rows), 0)
    line_s = lax.broadcasted_iota(jnp.int32, (rows, rows), 1)
    forget = fg_ref[...].astype(F32)
    logf = -(jnp.maximum(-forget, 0.0) + jnp.log1p(jnp.exp(-jnp.abs(forget))))
    gate = ig_ref[...].astype(F32)
    running = jnp.dot(
        logf, (line_t <= line_s).astype(F32),
        preferred_element_type=F32, precision=lax.Precision.HIGHEST,
    )
    brow[...] = running
    bcol[...] = running.T
    grow[...] = gate
    total = running[:, rows - 1 : rows]
    exponent = total - running + gate
    peak = jnp.max(exponent, axis=1, keepdims=True)
    wcol[...] = jnp.exp(exponent - peak).T
    own_h[:, dk : 2 * dk] = jnp.broadcast_to(peak, (heads, dk))
    own_h[:, 2 * dk :] = jnp.broadcast_to(total, (heads, dk))

    k_in.wait()

    def keys(h, carry):
        start = dequant(k_ref, 1, h, dk, kd)
        place = (slice(None), pl.ds(start, dk))
        weighted = (kd[place].astype(F32) * column(wcol, h)).astype(BF16)
        wk[place] = weighted
        own_h[pl.ds(h, 1), pl.ds(0, dk)] = jnp.sum(weighted.astype(F32), axis=0, keepdims=True)
        return carry

    lax.fori_loop(0, heads, keys, 0, unroll=2)

    def empty_header(ref):
        ref[:, 0:dk] = jnp.zeros((heads, dk), F32)
        ref[:, dk : 2 * dk] = jnp.full((heads, dk), NEG_FILL, F32)
        ref[:, 2 * dk :] = jnp.zeros((heads, dk), F32)

    @pl.when(z == 0)
    def _():
        empty_header(up_h)
        up_buf[...] = jnp.zeros_like(up_buf)

    @pl.when(c == 0)
    def _():
        empty_header(r_h)
        r_buf[...] = jnp.zeros_like(r_buf)

    def join(first, later, dst, at):
        m1, m2, f2 = first[:, dk : 2 * dk], later[:, dk : 2 * dk], later[:, 2 * dk :]
        m = jnp.maximum(m1 + f2, m2)
        w1, w2 = jnp.exp(m1 + f2 - m), jnp.exp(m2 - m)
        wts[at] = w1
        wts[at + 1] = w2
        dst[:, 0:dk] = w1 * first[:, 0:dk] + w2 * later[:, 0:dk]
        dst[:, dk : 2 * dk] = m
        dst[:, 2 * dk :] = first[:, 2 * dk :] + f2

    greeted = sum(there.astype(jnp.int32) for there, _ in greet)
    pl.semaphore_wait(barrier, greeted)

    @pl.when(has_down)
    def _():
        up_head.wait_recv()

    join(up_h, own_h, tot_h, 0)

    @pl.when(has_up)
    def _():
        up_head.start()

    def weight(at, h):
        return wts[at, pl.ds(h, 1), :][:, 0:pw]

    def local(h):
        start = dequant(q_ref, 0, h, dk, qd)
        place = (slice(None), pl.ds(start, dk))
        scores = lax.dot_general(
            qd[place], kd[place], (((1,), (1,)), ((), ())), preferred_element_type=F32
        ) * factor
        gaps = column(bcol, h) - brow[pl.ds(h, 1), :] + grow[pl.ds(h, 1), :]
        gaps = jnp.where(line_t >= line_s, gaps, NEG_FILL)
        top = jnp.max(gaps, axis=1, keepdims=True)
        product = jnp.exp(gaps - top) * scores
        peak_l[h] = jnp.broadcast_to(top, (rows, BLK))
        den_l[h] = jnp.broadcast_to(jnp.sum(product, axis=1, keepdims=True), (rows, BLK))
        inner[...] = product.astype(BF16)

    def local_values(h):
        wide = (slice(None), pl.ds(pl.multiple_of(h * dv, dv), dv))
        num[wide] = jnp.dot(inner[...], vd[wide], preferred_element_type=F32)

    def head_state(h):
        wide = (slice(None), pl.ds(pl.multiple_of(h * dv, dv), dv))
        found = lax.dot_general(
            wk[:, pl.ds(pl.multiple_of(h * dk, dk), dk)], vd[wide],
            (((0,), (0,)), ((), ())), preferred_element_type=F32,
        )
        for p in range(PIECES):
            state[p] = found[:, p * pw : (p + 1) * pw]

    def upward(i):
        h = lax.div(i, PIECES)

        @pl.when(has_down)
        def _():
            up_copy(i).wait_recv()

        mine = state[lax.rem(i, PIECES)]
        tot_buf[i] = (weight(0, h) * up_buf[i].astype(F32) + weight(1, h) * mine).astype(BF16)

        @pl.when(has_up)
        def _():
            up_copy(i).start()

    def ahead(i):
        h, p = lax.div(i, PIECES), lax.rem(i, PIECES)

        @pl.when(p == 0)
        def _():
            local(h)

        @pl.when(p == min(1, PIECES - 1))
        def _():
            local_values(h)

        @pl.when((p == PIECES - 2) & (h + 1 < heads))
        def _():
            dequant(v_ref, 2, h + 1, dv, vd)

        @pl.when((p == PIECES - 1) & (h + 1 < heads))
        def _():
            head_state(h + 1)

    def header_row():
        @pl.when(has_row)
        def _():
            down_head.wait_recv()

        @pl.when(has_row & has_down)
        def _():
            down_head.start()

        @pl.when(gives_row)
        def _():
            join(r_h, tot_h, rs_h, 2)
            row_head.start()

        join(r_h, up_h, own_h, 4)

    def forward(j):
        h = lax.div(j, PIECES)

        @pl.when(j == 0)
        def _():
            header_row()

        @pl.when(has_row)
        def _():
            down_copy(j).wait_recv()

        @pl.when(has_row & has_down)
        def _():
            down_copy(j).start()

        @pl.when(gives_row)
        def _():
            rs_buf[j] = (
                weight(2, h) * r_buf[j].astype(F32) + weight(3, h) * tot_buf[j].astype(F32)
            ).astype(BF16)
            row_copy(j).start()

    def finish(j):
        h = lax.div(j, PIECES)

        @pl.when(lax.rem(j, PIECES) == 0)
        def _():
            place = (slice(None), pl.ds(pl.multiple_of(h * dk, dk), dk))
            header = own_h[pl.ds(h, 1), :]
            norm, m = header[:, 0:dk], header[:, dk : dk + BLK]
            inter = column(bcol, h) + m
            top = jnp.maximum(peak_l[h], inter)
            shrink = jnp.exp(peak_l[h] - top)
            lift = jnp.exp(inter - top) * factor
            raised = (qd[place].astype(F32) * lift[:, 0:1]).astype(BF16)
            lifted[...] = raised
            den = shrink * den_l[h] + jnp.sum(raised.astype(F32) * norm, axis=1, keepdims=True)
            fin[0] = shrink
            fin[1] = 1.0 / jnp.maximum(jnp.abs(den), 1.0)

        piece = pl.ds(pl.multiple_of(j * pw, pw), pw)
        begin = (weight(4, h) * r_buf[j].astype(F32) + weight(5, h) * up_buf[j].astype(F32)).astype(BF16)
        above_line = num[:, piece] * fin[0][:, 0:1] + jnp.dot(
            lifted[...], begin, preferred_element_type=F32
        )
        out_ref[:, piece] = (above_line * fin[1][:, 0:1]).astype(BF16)

        @pl.when(lax.rem(j, PIECES) == PIECES - 1)
        def _():
            out_copy(h).start()

    def out_copy(h):
        wide = (slice(None), pl.ds(pl.multiple_of(h * dv, dv), dv))
        return pltpu.make_async_copy(out_ref.at[wide], out_any.at[wide], out_s.at[h])

    skew = Z_SKEW * (last - z) + C_SKEW * c
    v_in.wait()
    dequant(v_ref, 2, 0, dv, vd)
    head_state(0)
    q_in.wait()

    def step(t, carry):
        @pl.when(t < pieces)
        def _():
            upward(t)

        @pl.when((t >= skew) & (t < pieces + skew))
        def _():
            forward(t - skew)

        @pl.when(t < pieces)
        def _():
            ahead(t)

        @pl.when(t > skew)
        def _():
            finish(t - skew - 1)

        return carry

    lax.fori_loop(0, pieces + skew + 1, step, 0)

    @pl.when(has_up)
    def _():
        up_head.wait_send()

    @pl.when(has_row & has_down)
    def _():
        down_head.wait_send()

    @pl.when(gives_row)
    def _():
        row_head.wait_send()

    def drain_out(h, carry):
        out_copy(h).wait()
        return carry

    lax.fori_loop(0, heads, drain_out, 0)

    def drain(i, carry):
        @pl.when(has_up)
        def _():
            up_copy(i).wait_send()

        @pl.when(has_row & has_down)
        def _():
            down_copy(i).wait_send()

        @pl.when(gives_row)
        def _():
            row_copy(i).wait_send()

        return carry

    lax.fori_loop(0, pieces, drain, 0)


def body(nc, nz, *args):
    rows = args[0].shape[0]
    heads = args[3].shape[2]
    dk, dv = args[0].shape[1] // heads, args[2].shape[1] // heads
    pieces, pw = heads * PIECES, dv // PIECES
    vmem, smem = pl.BlockSpec(memory_space=pltpu.VMEM), pl.BlockSpec(memory_space=pltpu.SMEM)
    passed = pltpu.VMEM((pieces, dk, pw), BF16)
    header = pltpu.VMEM((heads, 3 * dk), F32)
    sems = pltpu.SemaphoreType.DMA((pieces,))
    return pl.pallas_call(
        functools.partial(kernel, (heads, dk, dv, nc, nz)),
        out_shape=jax.ShapeDtypeStruct((rows, heads * dv), BF16),
        in_specs=[pl.BlockSpec(memory_space=pl.ANY)] * 3 + [smem] * 4 + [vmem] * 2,
        out_specs=pl.BlockSpec(memory_space=pl.ANY),
        scratch_shapes=[
            pltpu.VMEM((rows, heads * dv), BF16),
            pltpu.SemaphoreType.DMA((heads,)),
            pltpu.VMEM((rows, heads * dk), BF16),
            pltpu.VMEM((rows, heads * dk), BF16),
            pltpu.VMEM((rows, heads * dv), BF16),
            pltpu.SemaphoreType.DMA((3,)),
            pltpu.VMEM((rows, heads * dk), BF16),
            pltpu.VMEM((rows, heads * dk), BF16),
            pltpu.VMEM((rows, heads * dv), BF16),
            pltpu.VMEM((rows, heads * dk), BF16),
            pltpu.VMEM((rows, heads * dv), F32),
            pltpu.VMEM((PIECES, dk, pw), F32),
            pltpu.VMEM((rows, dk), BF16),
            pltpu.VMEM((rows, rows), BF16),
            passed,
            passed,
            passed,
            passed,
            pltpu.VMEM((rows, heads), F32),
            pltpu.VMEM((rows, heads), F32),
            pltpu.VMEM((heads, rows), F32),
            pltpu.VMEM((heads, rows), F32),
            pltpu.VMEM((heads, rows, BLK), F32),
            pltpu.VMEM((heads, rows, BLK), F32),
            pltpu.VMEM((2, rows, BLK), F32),
            header,
            header,
            header,
            header,
            header,
            pltpu.VMEM((6, heads, dk), F32),
            sems,
            sems,
            sems,
            sems,
            sems,
            pltpu.SemaphoreType.DMA((5,)),
        ],
        compiler_params=pltpu.CompilerParams(
            collective_id=0, has_side_effects=True, vmem_limit_bytes=60 * 1024 * 1024
        ),
    )(*args[:3], args[3].transpose(1, 0, 2), *args[4:7], args[7].T, args[8].T)


def solution(mesh):
    rows = ("grp", "ctx", "head")
    placed = tuple(P(rows, *([None] * (n - 1))) for n in (2, 2, 2, 3, 2, 2, 2, 2, 2))
    return jax.shard_map(
        functools.partial(body, mesh.shape["ctx"], mesh.shape["head"]),
        mesh=mesh, in_specs=placed, out_specs=P(rows, None), check_vma=False,
    )
```
